256 devices in a mesh: branch: 32 (over z, x), tensor: 8 (over y, core).
Axes of the slice: x: 4, y: 4, z: 8, core: 2. Of those that a mesh axis runs over, the one named last changes fastest.
Arguments:
- hidden: bfloat16 [4096, 4, 4096], P('branch', None, 'tensor'), may hold values from -6 to 6
- gain: float32 [4096], replicated, may hold values from 0.5 to 1.5
- w_query: bfloat16 [4096, 4096], P(None, 'tensor'), may hold values from -0.09375 to 0.09375
- w_keyval: bfloat16 [2, 4096, 1024], P(None, None, 'tensor'), may hold values from -0.09375 to 0.09375
- w_out: bfloat16 [4096, 4096], P('tensor'), may hold values from -0.09375 to 0.09375
- kv_codes: bfloat16 [1024, 2, 64, 1024], P('branch', None, None, 'tensor'), may hold values from -12 to 12
- kv_scales: bfloat16 [1024, 2, 8], P('branch', None, 'tensor'), may hold values from 0.5 to 24
- fork_export: int32 [256], P('branch'), may hold values from 0 to 31
- fork_pull: int32 [32, 64], replicated, may hold values from 0 to 255, as said below
- page_table: int32 [4096, 8], P('branch'), may hold values from 0 to 95
- lengths: int32 [4096], P('branch'), may hold values from 1 to 512, as said below
Outputs:
- mixed: bfloat16 [4096, 4, 4096], P('branch', None, 'tensor')
The draws below stay inside these ranges and needn't reach their ends.
Inputs may be any that keep to these rules, and one draw needn't show every extreme that they name: `fork_pull`: an entry s * 8 + e names offered page e of group s. In each row at most 4 entries name one group, and some group is named exactly 4 times in every row. `lengths`: some branch has exactly 512 tokens.
All inputs are finite; a program needn't handle non-finite values.
Results may differ from the reference program's by a relative error of at most 0.017.
Values may be sent and summed in bfloat16 or wider, within the bound.
No kernel may reach another device: no remote copies, remote signals or barrier semaphores. Data moves between devices by JAX's collectives and lax.ppermute only.
A program may use at most 128 MiB of HBM per device.

```python
import math
import jax
import jax.numpy as jnp
from jax import lax

D = 4096
HEADS = 32
KVH = 8
HD = 128
PAGE = 64
STEPS = 4
BR_DEV = 128
MAXP = 8
OWN_PAGES = 32
FORK_DEV = 64
EXPORT = 8
CAP = 4
BRANCHES = 4096
POOL_PAGES = 1024
EXPORTS = 256
N_BRANCH = 32
N_TENSOR = 8


def draw_kv_scales(key, part):
    key = jax.random.fold_in(key, 11)
    shape = (N_BRANCH * OWN_PAGES, 2, KVH)
    base = jnp.exp(jax.random.uniform(key, shape, jnp.float32, math.log(0.5), math.log(2.0)))
    return base.astype(jnp.bfloat16)


def draw_fork_pull(key, part):
    key = jax.random.fold_in(key, 17)
    row_keys = jax.random.split(key, N_BRANCH)

    def one_row(row_key):
        order = jax.random.permutation(row_key, N_BRANCH).astype(jnp.int32)
        source = order[jnp.arange(FORK_DEV) // CAP]
        entry = jax.random.randint(jax.random.fold_in(row_key, 1), (FORK_DEV,), 0, EXPORT)
        return (source * EXPORT + entry).astype(jnp.int32)
    return jax.vmap(one_row)(row_keys)


def draw_lengths(key, part):
    key = jax.random.fold_in(key, 23)
    most = MAXP * PAGE
    total = N_BRANCH * BR_DEV
    group_top = jax.random.randint(jax.random.fold_in(key, 1), (N_BRANCH,), most // 4 + 1, most + 1)
    tops = jnp.repeat(group_top, BR_DEV)
    values = jax.random.randint(key, (total,), 1, tops + 1)
    spot = jax.random.randint(jax.random.fold_in(key, 2), (), 0, total)
    return jnp.where(jnp.arange(total) == spot, most, values).astype(jnp.int32)


def plant(drawn, rng, low, top_value):
    shape = drawn.shape
    place = [jax.random.randint(jax.random.fold_in(rng, axis), (), 0, shape[axis]) for axis in range(len(shape))]
    drawn = drawn.at[tuple(place)].set(low)
    longest = shape.index(max(shape))
    place[longest] = (place[longest] + 1) % shape[longest]
    return drawn.at[tuple(place)].set(top_value)


def level_of(stream_key, dims, cuts, smallest, top_value):
    level = 1.0
    for position, parts in cuts:
        steps = jax.random.uniform(jax.random.fold_in(jax.random.fold_in(stream_key, 6), position), (parts,), jnp.float32, smallest / len(cuts), top_value / len(cuts))
        level = level * jnp.repeat(jnp.exp(steps), dims[position] // parts).reshape((-1,) + (1,) * (len(dims) - 1 - position))
    return level


def centred(stream_key, dims, deviation, bound, cuts=(), kind=jnp.bfloat16):
    loudness = level_of(stream_key, dims, cuts, -0.22, 0.18) if cuts else 1.0
    values = jax.random.normal(stream_key, dims, jnp.float32) * deviation * loudness
    return jnp.minimum(jnp.maximum(values, -bound), bound).astype(kind)


def setup_inputs(seed: int = 0) -> dict:
    key_list = jax.random.split(jax.random.key(seed), 12)
    hidden = centred(key_list[0], (BRANCHES, STEPS, D), 1.0, 6.0, ((0, 32), (2, 8)))
    gain = jnp.clip(1.0 + 0.1 * jax.random.normal(key_list[1], (D,), jnp.float32), 0.5, 1.5)
    w_query = centred(key_list[2], (D, HEADS * HD), D ** -0.5, 0.09375, ((1, 8),))
    w_keyval = centred(key_list[3], (2, D, KVH * HD), D ** -0.5, 0.09375, ((2, 8),))
    w_out = centred(key_list[4], (HEADS * HD, D), (HEADS * HD) ** -0.5, 0.09375, ((0, 8),))
    kv_codes = centred(key_list[5], (POOL_PAGES, 2, PAGE, KVH * HD), 2.0, 12.0, ((0, 32), (3, 8)))
    kv_scales = draw_kv_scales(jax.random.fold_in(key_list[11], 71), 0)
    fork_export = plant(jax.random.randint(key_list[7], (EXPORTS,), 0, OWN_PAGES), jax.random.fold_in(key_list[7], 1), 0, OWN_PAGES - 1).astype(jnp.int32)
    fork_pull = draw_fork_pull(jax.random.fold_in(key_list[11], 71), 0)
    page_table = plant(jax.random.randint(key_list[9], (BRANCHES, MAXP), 0, FORK_DEV + OWN_PAGES), jax.random.fold_in(key_list[9], 1), 0, (FORK_DEV + OWN_PAGES) - 1).astype(jnp.int32)
    lengths = draw_lengths(jax.random.fold_in(key_list[11], 71), 0)
    return dict(hidden=hidden, gain=gain, w_query=w_query, w_keyval=w_keyval, w_out=w_out, kv_codes=kv_codes, kv_scales=kv_scales, fork_export=fork_export, fork_pull=fork_pull, page_table=page_table, lengths=lengths)


def rotate(values, positions):
    half = values.shape[-1] // 2
    freq = jnp.exp(-(2.0 * jnp.arange(half).astype(jnp.float32) / values.shape[-1]) * math.log(500000.0))
    angle = positions.astype(jnp.float32)[:, None] * freq[None, :]
    cosine = jnp.cos(angle)[:, None, :]
    sine = jnp.sin(angle)[:, None, :]
    first = values[..., :half]
    second = values[..., half:]
    return jnp.concatenate([first * cosine - second * sine, second * cosine + first * sine], axis=-1)

def attend_block(query, key_new, value_new, codes, scales, lengths_block):
    blocks, slots, page = (codes.shape[0], codes.shape[1], codes.shape[3])
    heads_here = query.shape[2]
    steps = query.shape[1]
    keys = codes[:, :, 0].reshape(blocks, slots, page, heads_here, HD).astype(jnp.float32)
    values = codes[:, :, 1].reshape(blocks, slots, page, heads_here, HD).astype(jnp.float32)
    key_scale = jnp.transpose(scales[:, :, 0].astype(jnp.float32), (0, 2, 1))[:, None, :, None, :, None]
    value_scale = jnp.transpose(scales[:, :, 1].astype(jnp.float32), (0, 2, 1))[:, None, :, None, :, None]
    query_f = query.astype(jnp.float32)
    context = jnp.einsum('bthgd,bmphd->bthgmp', query_f, keys) * key_scale
    token = jnp.arange(slots).astype(jnp.int32)[:, None] * page + jnp.arange(page).astype(jnp.int32)[None, :]
    live = (token[None, :, :] < lengths_block[:, None, None])[:, None, None, None, :, :]
    fresh = jnp.einsum('bthgd,bshd->bthgs', query_f, key_new.astype(jnp.float32))
    causal = (jnp.arange(steps)[:, None] >= jnp.arange(steps)[None, :])[None, :, None, None, :]
    context = jnp.where(live, context, -1e+30)
    fresh = jnp.where(causal, fresh, -1e+30)
    top = jnp.maximum(lax.optimization_barrier(jnp.max(context, axis=(4, 5))), lax.optimization_barrier(jnp.max(fresh, axis=4)))
    context_exp = jnp.where(live, jnp.exp(context - top[..., None, None]), 0.0)
    fresh_exp = jnp.where(causal, jnp.exp(fresh - top[..., None]), 0.0)
    total = lax.optimization_barrier(jnp.sum(context_exp, axis=(4, 5))) + lax.optimization_barrier(jnp.sum(fresh_exp, axis=4))
    context_w = (context_exp / total[..., None, None] * value_scale).astype(jnp.bfloat16)
    fresh_w = (fresh_exp / total[..., None]).astype(jnp.bfloat16)
    result = jnp.einsum('bthgmp,bmphd->bthgd', context_w.astype(jnp.float32), values)
    result = result + jnp.einsum('bthgs,bshd->bthgd', fresh_w.astype(jnp.float32), value_new.astype(jnp.float32))
    return result.astype(jnp.bfloat16)

def reference(hidden, gain, w_query, w_keyval, w_out, kv_codes, kv_scales, fork_export, fork_pull, page_table, lengths):
    branches = hidden.shape[0]
    group = HEADS // KVH
    rows = hidden.astype(jnp.float32).reshape(branches * STEPS, D)
    power = lax.optimization_barrier(jnp.mean(rows * rows, axis=-1, keepdims=True))
    normed = (rows * lax.rsqrt(power + 1e-05) * gain).astype(jnp.bfloat16)
    positions = (lengths[:, None] + jnp.arange(STEPS).astype(jnp.int32)[None, :]).reshape(-1)
    query = jnp.dot(normed, w_query, preferred_element_type=jnp.float32).reshape(-1, HEADS, HD)
    query = (rotate(query, positions) * HD ** (-0.5)).astype(jnp.bfloat16).reshape(branches, STEPS, KVH, group, HD)
    key_new = jnp.dot(normed, w_keyval[0], preferred_element_type=jnp.float32).reshape(-1, KVH, HD)
    key_new = rotate(key_new, positions).astype(jnp.bfloat16).reshape(branches, STEPS, KVH, HD)
    value_new = jnp.dot(normed, w_keyval[1], preferred_element_type=jnp.float32).astype(jnp.bfloat16).reshape(branches, STEPS, KVH, HD)
    parents = fork_pull // EXPORT * OWN_PAGES + fork_export[fork_pull]
    owned = jnp.arange(N_BRANCH).astype(jnp.int32)[:, None] * OWN_PAGES + jnp.arange(OWN_PAGES).astype(jnp.int32)[None, :]
    pool = jnp.concatenate([parents.astype(jnp.int32), owned], axis=1)
    owner = jnp.arange(branches).astype(jnp.int32) // BR_DEV
    context = pool[owner[:, None], page_table]
    block = 8
    count = branches // block

    def shaped(array):
        return array.reshape((count, block) + array.shape[1:])

    def one_block(items):
        pages, lens, query_b, key_b, value_b = items
        return attend_block(query_b, key_b, value_b, kv_codes[pages], kv_scales[pages], lens)
    attended = lax.map(one_block, (shaped(context), shaped(lengths), shaped(query), shaped(key_new), shaped(value_new)))
    attended = attended.reshape(branches * STEPS, HEADS * HD)
    inner = HEADS * HD // N_TENSOR
    total = jnp.zeros((branches * STEPS, D), jnp.float32)
    for index in range(N_TENSOR):
        partial_sum = jnp.dot(attended[:, index * inner:(index + 1) * inner], w_out[index * inner:(index + 1) * inner], preferred_element_type=jnp.float32).astype(jnp.bfloat16)
        partial_sum = lax.optimization_barrier(partial_sum)
        total = total + partial_sum.astype(jnp.float32)
    return total.astype(jnp.bfloat16).reshape(branches, STEPS, D)
```

```python
import functools
import math

import jax
import jax.numpy as jnp
from jax import lax
from jax.experimental import pallas as pl
from jax.experimental.pallas import tpu as pltpu
from jax.sharding import PartitionSpec as P

HEADS = 32
KVH = 8
HD = 128
PAGE = 64
MAXP = 8
STEPS = 4
GROUP = HEADS // KVH
OWN = 32
FORK = 64
EXPORT = 8
NZ, NX, NY = 8, 4, 4
ROWS = GROUP * STEPS
KPART = EXPORT * PAGE + 16
VPART = EXPORT * PAGE
KOWN = NZ * NX * KPART
VOWN = NZ * NX * VPART
BLOCK = 16
NEG = -1e30
LIMIT = 56 * 1024 * 1024


def from_z(value, d):
    perm = [(z * NX + x, ((z - d) % NZ) * NX + x) for z in range(NZ) for x in range(NX)]
    return lax.ppermute(value, "branch", perm)


def from_x(value, d):
    perm = [(z * NX + x, z * NX + (x - d) % NX) for z in range(NZ) for x in range(NX)]
    return lax.ppermute(value, "branch", perm)


def from_y(value, d):
    perm = [(y * 2 + c, ((y - d) % NY) * 2 + c) for y in range(NY) for c in range(2)]
    return lax.ppermute(value, "tensor", perm)


def from_core(value):
    return lax.ppermute(value, "tensor", [(t, t ^ 1) for t in range(2 * NY)])


def spec(space):
    return pl.BlockSpec(memory_space=space)


def export_kernel(picks, scales, codes, key_out, value_out, sems):
    copies = []
    for e in range(EXPORT):
        page = picks[e]
        for kind, out in enumerate((key_out, value_out)):
            copies.append(
                pltpu.make_async_copy(
                    codes.at[page, kind], out.at[pl.ds(e * PAGE, PAGE), :], sems.at[2 * e + kind]
                )
            )
            copies[-1].start()
    place = lax.broadcasted_iota(jnp.int32, (16, HD), 0)
    rows = jnp.zeros((16, HD), jnp.float32)
    for e in range(EXPORT):
        for kind in range(2):
            rows = jnp.where(place == kind * EXPORT + e, scales[picks[e] * 2 + kind], rows)
    key_out[pl.ds(VPART, 16), :] = rows.astype(jnp.bfloat16)
    for copy in copies:
        copy.wait()


def export_pages(codes, scales, picks):
    return pl.pallas_call(
        export_kernel,
        out_shape=(
            jax.ShapeDtypeStruct((KPART, HD), jnp.bfloat16),
            jax.ShapeDtypeStruct((VPART, HD), jnp.bfloat16),
        ),
        in_specs=[spec(pltpu.SMEM), spec(pltpu.SMEM), spec(pl.ANY)],
        out_specs=(spec(pltpu.VMEM), spec(pltpu.VMEM)),
        scratch_shapes=[pltpu.SemaphoreType.DMA((2 * EXPORT,))],
        name="export_pages",
    )(picks, scales, codes)


def project_kernel(place, *refs):
    parts = refs[:8]
    gain, w_query, w_keyval, cosine, sine, q_out, k_out, v_out, qf = refs[8:]
    y, c = place[0], place[1]
    rows = parts[0].shape[0]
    width = parts[0].shape[1]
    power = jnp.zeros((rows, 1), jnp.float32)
    acc_q = jnp.zeros((rows, GROUP * HD), jnp.float32)
    acc_k = jnp.zeros((rows, HD), jnp.float32)
    acc_v = jnp.zeros((rows, HD), jnp.float32)
    for index, part in enumerate(parts):
        core = c if index < NY else 1 - c
        t = lax.rem(y + index % NY, NY) * 2 + core
        feats = part[...].astype(jnp.float32)
        power = power + jnp.sum(feats * feats, axis=1, keepdims=True)
        scaled = (feats * gain[pl.ds(t, 1), :]).astype(jnp.bfloat16)
        here = pl.ds(pl.multiple_of(t * width, width), width)
        acc_q = acc_q + jnp.dot(scaled, w_query[here, :], preferred_element_type=jnp.float32)
        acc_k = acc_k + jnp.dot(scaled, w_keyval[0, here, :], preferred_element_type=jnp.float32)
        acc_v = acc_v + jnp.dot(scaled, w_keyval[1, here, :], preferred_element_type=jnp.float32)
    norm = lax.rsqrt(power / (width * 8) + 1e-05)
    cos, sin = cosine[...], sine[...]

    def rope(v):
        return v * cos + pltpu.roll(v, HD // 2, 1) * sin

    for g in range(GROUP):
        head = rope(acc_q[:, g * HD : (g + 1) * HD] * norm) * HD ** (-0.5)
        qf[pl.ds(g, rows, stride=GROUP), :] = head
    q_out[...] = qf[...].astype(jnp.bfloat16)
    k_out[...] = rope(acc_k * norm).astype(jnp.bfloat16)
    v_out[...] = (acc_v * norm).astype(jnp.bfloat16)


def project(place, parts, gain, w_query, w_keyval, cosine, sine):
    rows = parts[0].shape[0]
    return pl.pallas_call(
        project_kernel,
        out_shape=(
            jax.ShapeDtypeStruct((rows * GROUP, HD), jnp.bfloat16),
            jax.ShapeDtypeStruct((rows, HD), jnp.bfloat16),
            jax.ShapeDtypeStruct((rows, HD), jnp.bfloat16),
        ),
        in_specs=[spec(pltpu.SMEM)] + [spec(pltpu.VMEM)] * 13,
        out_specs=(spec(pltpu.VMEM),) * 3,
        scratch_shapes=[pltpu.VMEM((rows * GROUP, HD), jnp.float32)],
        compiler_params=pltpu.CompilerParams(vmem_limit_bytes=LIMIT),
        name="project",
    )(place, *parts, gain, w_query, w_keyval, cosine, sine)


def attend_kernel(first, count, n_keys, n_values, place, table, krow, vrow, prow, lens, *refs):
    q, k_new, v_new, own_scales = refs[:4]
    keys = refs[4 : 4 + n_keys]
    values = refs[4 + n_keys : 4 + n_keys + n_values]
    (w_out, sib_out, own_out, kpool, vpool, wbuf, ksc, vsc, score, fresh_acc, inverse, result,
     ksems, vsems, wsem) = refs[4 + n_keys + n_values :]

    def copies(parts, pool, sems):
        made, at = [], 0
        for i, part in enumerate(parts):
            n = part.shape[0]
            made.append(pltpu.make_async_copy(part, pool.at[pl.ds(at, n), :], sems.at[i]))
            at += n
        return made

    key_copies = copies(keys, kpool, ksems)
    value_copies = copies(values, vpool, vsems)
    w_copy = pltpu.make_async_copy(w_out, wbuf, wsem)
    for copy in key_copies + value_copies + [w_copy]:
        copy.start()
    for copy in key_copies:
        copy.wait()
    for part in range(NZ * NX):
        both = kpool[pl.ds(part * KPART + VPART, 16), :].astype(jnp.float32)
        ksc[pl.ds(part * EXPORT, EXPORT), :] = both[:EXPORT]
        vsc[pl.ds(part * EXPORT, EXPORT), :] = both[EXPORT:]
    mine = own_scales[...].astype(jnp.float32)
    ksc[pl.ds(NZ * NX * EXPORT, OWN), :] = mine[:OWN]
    vsc[pl.ds(NZ * NX * EXPORT, OWN), :] = mine[OWN:]
    for copy in value_copies:
        copy.wait()

    rows = BLOCK * ROWS
    span = 4 * PAGE
    lane = lax.broadcasted_iota(jnp.int32, (1, HD), 1)
    token = lax.broadcasted_iota(jnp.int32, (ROWS, span), 1)

    def scale_row(ref, slots):
        pieces = []
        for m in range(0, len(slots), 2):
            left = ref[pl.ds(prow[slots[m]], 1), :]
            right = ref[pl.ds(prow[slots[m + 1]], 1), :]
            pieces.append(jnp.where(lane < PAGE, left, right))
        return jnp.concatenate(pieces, axis=1)

    def pages(pool, where, slots):
        return jnp.concatenate(
            [pool[pl.ds(pl.multiple_of(where[s], 16), PAGE), :] for s in slots], axis=0
        )

    def one_block(block, carry):
        base = block * BLOCK
        queries = q[pl.ds(pl.multiple_of(block * rows, rows), rows), :]
        for i in range(BLOCK):
            branch = first + base + i
            length = lens[branch]
            for half in range(2):
                slots = [table[branch * MAXP + half * 4 + m] for m in range(4)]
                s = lax.dot_general(
                    queries[i * ROWS : (i + 1) * ROWS],
                    pages(kpool, krow, slots),
                    (((1,), (1,)), ((), ())),
                    preferred_element_type=jnp.float32,
                )
                live = token < length - half * span
                score[pl.ds(i * ROWS, ROWS), pl.ds(half * span, span)] = jnp.where(
                    live, s * scale_row(ksc, slots), NEG
                )
        new = pl.ds(pl.multiple_of(base * STEPS, BLOCK * STEPS), BLOCK * STEPS)
        fresh = lax.dot_general(
            queries, k_new[new, :], (((1,), (1,)), ((), ())), preferred_element_type=jnp.float32
        )
        row = lax.broadcasted_iota(jnp.int32, fresh.shape, 0)
        col = lax.broadcasted_iota(jnp.int32, fresh.shape, 1)
        step = lax.shift_right_logical(row, 2)
        same = lax.shift_right_logical(step, 2) == lax.shift_right_logical(col, 2)
        fresh = jnp.where(same & ((step & 3) >= (col & 3)), fresh, NEG)
        context = score[...]
        top = jnp.maximum(
            jnp.max(context, axis=1, keepdims=True), jnp.max(fresh, axis=1, keepdims=True)
        )
        context = jnp.exp(context - top)
        fresh = jnp.exp(fresh - top)
        total = jnp.sum(context, axis=1, keepdims=True) + jnp.sum(fresh, axis=1, keepdims=True)
        score[...] = context
        inverse[...] = jnp.broadcast_to(1.0 / total, inverse.shape)
        fresh_acc[...] = jnp.dot(
            fresh.astype(jnp.bfloat16), v_new[new, :], preferred_element_type=jnp.float32
        )
        for i in range(BLOCK):
            branch = first + base + i
            slots = [table[branch * MAXP + m] for m in range(MAXP)]
            here = pl.ds(i * ROWS, ROWS)
            weights = (score[here, :] * scale_row(vsc, slots)).astype(jnp.bfloat16)
            out = jnp.dot(weights, pages(vpool, vrow, slots), preferred_element_type=jnp.float32)
            there = pl.ds(pl.multiple_of(block * rows + i * ROWS, ROWS), ROWS)
            result[there, :] = (out + fresh_acc[here, :]) * inverse[here, :]
        return carry

    lax.fori_loop(0, count // BLOCK, one_block, 0)
    tokens = count * STEPS
    attended = jnp.concatenate(
        [result[pl.ds(g, tokens, stride=GROUP), :] for g in range(GROUP)], axis=1
    ).astype(jnp.bfloat16)
    w_copy.wait()
    y, c = place[0], place[1]
    width = sib_out.shape[2]
    for j in range(NY):
        for out, core in ((sib_out, 1 - c), (own_out, c)):
            t = lax.rem(y + j, NY) * 2 + core
            columns = wbuf[:, pl.ds(pl.multiple_of(t * width, width), width)]
            out[j] = jnp.dot(attended, columns, preferred_element_type=jnp.float32).astype(
                jnp.bfloat16
            )


def attend(first, count, place, table, maps, lens, q, k_new, v_new, own_scales, keys, values, w_out):
    tokens = count * STEPS
    inner, wide = w_out.shape
    width = wide // (2 * NY)
    n_pages = NZ * NX * EXPORT + OWN
    krows = sum(k.shape[0] for k in keys)
    vrows = sum(v.shape[0] for v in values)
    out = jax.ShapeDtypeStruct((NY, tokens, width), jnp.bfloat16)
    return pl.pallas_call(
        functools.partial(attend_kernel, first, count, len(keys), len(values)),
        out_shape=(out, out),
        in_specs=[spec(pltpu.SMEM)] * 6
        + [spec(pltpu.VMEM)] * 4
        + [spec(pl.ANY)] * (len(keys) + len(values) + 1),
        out_specs=(spec(pltpu.VMEM),) * 2,
        scratch_shapes=[
            pltpu.VMEM((krows, HD), jnp.bfloat16),
            pltpu.VMEM((vrows, HD), jnp.bfloat16),
            pltpu.VMEM((inner, wide), jnp.bfloat16),
            pltpu.VMEM((n_pages, HD), jnp.float32),
            pltpu.VMEM((n_pages, HD), jnp.float32),
            pltpu.VMEM((BLOCK * ROWS, MAXP * PAGE), jnp.float32),
            pltpu.VMEM((BLOCK * ROWS, HD), jnp.float32),
            pltpu.VMEM((BLOCK * ROWS, HD), jnp.float32),
            pltpu.VMEM((count * ROWS, HD), jnp.float32),
            pltpu.SemaphoreType.DMA((len(keys),)),
            pltpu.SemaphoreType.DMA((len(values),)),
            pltpu.SemaphoreType.DMA,
        ],
        compiler_params=pltpu.CompilerParams(vmem_limit_bytes=LIMIT),
        name="attend",
    )(place, table, *maps, lens, q, k_new, v_new, own_scales, *keys, *values, w_out)


def share_keys(part):
    held = {0: part}
    for d in range(1, 4):
        held[d] = from_z(held[d - 1], 1)
        held[-d] = from_z(held[1 - d], -1)
    held[4] = from_z(held[3], 1)
    here = jnp.concatenate([held[d] for d in (0, 1, 2, 3, 4, -3, -2, -1)], axis=0)
    right = from_x(here, 1)
    left = from_x(here, -1)
    half = here.shape[0] // 2
    far = [from_x(right[:half], 1), from_x(left[half:], -1)]
    return [here, right, *far, left]


def share_values(part):
    right = from_x(part, 1)
    left = from_x(part, -1)
    half = part.shape[0] // 2
    far = [from_x(right[:half], 1), from_x(left[half:], -1)]
    held = {0: jnp.concatenate([part, right, *far, left], axis=0)}
    for d in range(1, 4):
        held[d] = from_z(held[d - 1], 1)
        held[-d] = from_z(held[1 - d], -1)
    half = held[0].shape[0] // 2
    far = [from_z(held[3][:half], 1), from_z(held[-3][half:], -1)]
    return [held[0], held[1], held[2], held[3], *far, held[-3], held[-2], held[-1]]


def per_device(
    hidden,
    gain,
    w_query,
    w_keyval,
    w_out,
    kv_codes,
    kv_scales,
    fork_export,
    fork_pull,
    page_table,
    lengths,
):
    branches, steps, width = hidden.shape
    rows = branches * steps
    tensor = lax.axis_index("tensor")
    myself = lax.axis_index("branch")
    place = jnp.stack([tensor // 2, tensor % 2]).astype(jnp.int32)

    flat_scales = kv_scales.astype(jnp.float32).reshape(-1)
    key_part, value_part = export_pages(kv_codes, flat_scales, fork_export)
    keys = share_keys(key_part)
    values = share_values(value_part)

    own = hidden.reshape(rows, width)
    parts = [own, from_y(own, 1), from_y(own, 2), from_y(own, 3)]
    parts = parts + [from_core(part) for part in parts]

    half = HD // 2
    freq = jnp.exp(-(2.0 * jnp.arange(half).astype(jnp.float32) / HD) * math.log(500000.0))
    positions = (lengths[:, None] + jnp.arange(steps, dtype=jnp.int32)[None, :]).reshape(-1)
    angle = positions.astype(jnp.float32)[:, None] * freq[None, :]
    cos, sin = jnp.cos(angle), jnp.sin(angle)
    cosine = jnp.concatenate([cos, cos], axis=1)
    sine = jnp.concatenate([-sin, sin], axis=1)
    q, k_new, v_new = project(
        place, parts, gain.reshape(2 * NY, width), w_query, w_keyval, cosine, sine
    )

    pull = lax.dynamic_index_in_dim(fork_pull, myself, 0, keepdims=False)
    source, entry = pull // EXPORT, pull % EXPORT
    dz = (source // NX - myself // NX) % NZ
    dx = (source % NX - myself % NX) % NX
    mine = jnp.arange(OWN, dtype=jnp.int32)
    krow = jnp.concatenate([(dx * NZ + dz) * KPART + entry * PAGE, KOWN + mine * PAGE])
    vrow = jnp.concatenate([(dz * NX + dx) * VPART + entry * PAGE, VOWN + mine * PAGE])
    prow = jnp.concatenate([(dx * NZ + dz) * EXPORT + entry, NZ * NX * EXPORT + mine])
    maps = [m.astype(jnp.int32) for m in (krow, vrow, prow)]

    keys = keys + [kv_codes[:, 0].reshape(OWN * PAGE, HD)]
    values = values + [kv_codes[:, 1].reshape(OWN * PAGE, HD)]
    own_scales = jnp.broadcast_to(
        jnp.transpose(kv_scales, (1, 0, 2)).reshape(2 * OWN, 1), (2 * OWN, HD)
    )
    table = page_table.reshape(-1)

    chunks = 2
    count = branches // chunks
    outs = []
    for index in range(chunks):
        first = index * count
        sib, near = attend(
            first,
            count,
            place,
            table,
            maps,
            lengths,
            q[first * ROWS : (first + count) * ROWS],
            k_new[first * steps : (first + count) * steps],
            v_new[first * steps : (first + count) * steps],
            own_scales,
            keys,
            values,
            w_out,
        )
        got = from_core(sib)
        total = near.astype(jnp.float32) + got.astype(jnp.float32)
        sent = [total[j].astype(jnp.bfloat16) for j in range(NY)]
        summed = (
            total[0]
            + from_y(sent[1], -1).astype(jnp.float32)
            + from_y(sent[2], -2).astype(jnp.float32)
            + from_y(sent[3], -3).astype(jnp.float32)
        )
        outs.append(summed.astype(jnp.bfloat16).reshape(count, steps, width))
    return jnp.concatenate(outs, axis=0)


def solution(mesh):
    return jax.shard_map(
        per_device,
        mesh=mesh,
        in_specs=(
            P("branch", None, "tensor"),
            P(),
            P(None, "tensor"),
            P(None, None, "tensor"),
            P("tensor", None),
            P("branch", None, None, "tensor"),
            P("branch", None, "tensor"),
            P("branch"),
            P(),
            P("branch", None),
            P("branch"),
        ),
        out_specs=P("branch", None, "tensor"),
        check_vma=False,
    )
```

```python
import functools
import math

import jax
import jax.numpy as jnp
from jax import lax
from jax.experimental import pallas as pl
from jax.experimental.pallas import tpu as pltpu
from jax.sharding import PartitionSpec as P

HEADS = 32
KVH = 8
HD = 128
PAGE = 64
MAXP = 8
STEPS = 4
GROUP = HEADS // KVH
OWN = 32
FORK = 64
EXPORT = 8
NZ, NX, NY = 8, 4, 4
ROWS = GROUP * STEPS
CODES = EXPORT * PAGE
PART = 2 * CODES + 16
TAKE = NZ * 4
FAR = NZ * PART
KPACK = TAKE * PAGE + 2 * TAKE
VPACK = TAKE * PAGE
KOWN = FAR + (NX - 1) * KPACK
VOWN = FAR + (NX - 1) * VPACK
SFAR = NZ * EXPORT
SOWN = SFAR + (NX - 1) * TAKE
BLOCK = 16
NEG = -1e30
LIMIT = 30 * 1024 * 1024


def from_z(value, d, name="z"):
    perm = [(z * NX + x, ((z - d) % NZ) * NX + x) for z in range(NZ) for x in range(NX)]
    with jax.named_scope(name):
        return lax.ppermute(value, "branch", perm)


def from_x(value, d, name="x"):
    perm = [(z * NX + x, z * NX + (x - d) % NX) for z in range(NZ) for x in range(NX)]
    with jax.named_scope(name):
        return lax.ppermute(value, "branch", perm)


def from_y(value, d, name="y"):
    perm = [(y * 2 + c, ((y - d) % NY) * 2 + c) for y in range(NY) for c in range(2)]
    with jax.named_scope(name):
        return lax.ppermute(value, "tensor", perm)


def from_core(value, name="core"):
    with jax.named_scope(name):
        return lax.ppermute(value, "tensor", [(t, t ^ 1) for t in range(2 * NY)])


def spec(space):
    return pl.BlockSpec(memory_space=space)


def export_kernel(picks, scales, codes, out, sems):
    copies = []
    for e in range(EXPORT):
        page = picks[e]
        for kind in range(2):
            rows = pl.ds(kind * CODES + e * PAGE, PAGE)
            copies.append(
                pltpu.make_async_copy(codes.at[page, kind], out.at[rows, :], sems.at[2 * e + kind])
            )
            copies[-1].start()
    place = lax.broadcasted_iota(jnp.int32, (16, HD), 0)
    rows = jnp.zeros((16, HD), jnp.float32)
    for e in range(EXPORT):
        for kind in range(2):
            rows = jnp.where(place == kind * EXPORT + e, scales[picks[e] * 2 + kind], rows)
    out[pl.ds(2 * CODES, 16), :] = rows.astype(jnp.bfloat16)
    for copy in copies:
        copy.wait()


def export_pages(codes, scales, picks):
    return pl.pallas_call(
        export_kernel,
        out_shape=jax.ShapeDtypeStruct((PART, HD), jnp.bfloat16),
        in_specs=[spec(pltpu.SMEM), spec(pltpu.SMEM), spec(pl.ANY)],
        out_specs=spec(pltpu.VMEM),
        scratch_shapes=[pltpu.SemaphoreType.DMA((2 * EXPORT,))],
        name="export_pages",
    )(picks, scales, codes)


def pack_kernel(kind, rows, marks, *refs):
    parts, outs = refs[:NZ], refs[NZ : NZ + NX - 1]
    pool, ksc, vsc, kout, vout, sems = refs[NZ + NX - 1 :]
    copies = load(parts, pool, sems)
    for copy in copies:
        copy.wait()
    for i in range(NZ):
        both = pool[pl.ds(i * PART + 2 * CODES, 16), :].astype(jnp.float32)
        ksc[pl.ds(i * EXPORT, EXPORT), :] = both[:EXPORT]
        vsc[pl.ds(i * EXPORT, EXPORT), :] = both[EXPORT:]
    for d, out in enumerate(outs):
        for k in range(TAKE):
            row = pl.multiple_of(rows[d * TAKE + k] + kind * CODES, 16)
            out[pl.ds(k * PAGE, PAGE), :] = pool[pl.ds(row, PAGE), :]
        if kind == 0:
            for k in range(TAKE):
                mark = marks[d * TAKE + k]
                kout[pl.ds(k, 1), :] = ksc[pl.ds(mark, 1), :]
                vout[pl.ds(k, 1), :] = vsc[pl.ds(mark, 1), :]
            out[pl.ds(TAKE * PAGE, TAKE), :] = kout[...].astype(jnp.bfloat16)
            out[pl.ds(TAKE * PAGE + TAKE, TAKE), :] = vout[...].astype(jnp.bfloat16)


def pack(kind, rows, marks, parts):
    out = jax.ShapeDtypeStruct((VPACK if kind else KPACK, HD), jnp.bfloat16)
    return pl.pallas_call(
        functools.partial(pack_kernel, kind),
        out_shape=(out,) * (NX - 1),
        in_specs=[spec(pltpu.SMEM)] * 2 + [spec(pl.ANY)] * NZ,
        out_specs=(spec(pltpu.VMEM),) * (NX - 1),
        scratch_shapes=[
            pltpu.VMEM((NZ * PART, HD), jnp.bfloat16),
            pltpu.VMEM((SFAR, HD), jnp.float32),
            pltpu.VMEM((SFAR, HD), jnp.float32),
            pltpu.VMEM((TAKE, HD), jnp.float32),
            pltpu.VMEM((TAKE, HD), jnp.float32),
            pltpu.SemaphoreType.DMA((NZ,)),
        ],
        name="pack",
    )(rows, marks, *parts)


def project_kernel(place, *refs):
    parts = refs[:8]
    gain, w_query, w_keyval, cosine, sine, q_out, k_out, v_out, qf = refs[8:]
    y, c = place[0], place[1]
    rows = parts[0].shape[0]
    width = parts[0].shape[1]
    power = jnp.zeros((rows, 1), jnp.float32)
    acc_q = jnp.zeros((rows, GROUP * HD), jnp.float32)
    acc_k = jnp.zeros((rows, HD), jnp.float32)
    acc_v = jnp.zeros((rows, HD), jnp.float32)
    for index, part in enumerate(parts):
        core = c if index < NY else 1 - c
        t = lax.rem(y + index % NY, NY) * 2 + core
        feats = part[...].astype(jnp.float32)
        power = power + jnp.sum(feats * feats, axis=1, keepdims=True)
        scaled = (feats * gain[pl.ds(t, 1), :]).astype(jnp.bfloat16)
        here = pl.ds(pl.multiple_of(t * width, width), width)
        acc_q = acc_q + jnp.dot(scaled, w_query[here, :], preferred_element_type=jnp.float32)
        acc_k = acc_k + jnp.dot(scaled, w_keyval[0, here, :], preferred_element_type=jnp.float32)
        acc_v = acc_v + jnp.dot(scaled, w_keyval[1, here, :], preferred_element_type=jnp.float32)
    norm = lax.rsqrt(power / (width * 8) + 1e-05)
    cos, sin = cosine[...], sine[...]

    def rope(v):
        return v * cos + pltpu.roll(v, HD // 2, 1) * sin

    for g in range(GROUP):
        head = rope(acc_q[:, g * HD : (g + 1) * HD] * norm) * HD ** (-0.5)
        qf[pl.ds(g, rows, stride=GROUP), :] = head
    q_out[...] = qf[...].astype(jnp.bfloat16)
    k_out[...] = rope(acc_k * norm).astype(jnp.bfloat16)
    v_out[...] = (acc_v * norm).astype(jnp.bfloat16)


def project(place, parts, gain, w_query, w_keyval, cosine, sine):
    rows = parts[0].shape[0]
    return pl.pallas_call(
        project_kernel,
        out_shape=(
            jax.ShapeDtypeStruct((rows * GROUP, HD), jnp.bfloat16),
            jax.ShapeDtypeStruct((rows, HD), jnp.bfloat16),
            jax.ShapeDtypeStruct((rows, HD), jnp.bfloat16),
        ),
        in_specs=[spec(pltpu.SMEM)] + [spec(pltpu.VMEM)] * 13,
        out_specs=(spec(pltpu.VMEM),) * 3,
        scratch_shapes=[pltpu.VMEM((rows * GROUP, HD), jnp.float32)],
        compiler_params=pltpu.CompilerParams(vmem_limit_bytes=LIMIT),
        name="project",
    )(place, *parts, gain, w_query, w_keyval, cosine, sine)


def load(parts, pool, sems):
    copies, at = [], 0
    for i, part in enumerate(parts):
        n = part.shape[0]
        copies.append(pltpu.make_async_copy(part, pool.at[pl.ds(at, n), :], sems.at[i]))
        copies[-1].start()
        at += n
    return copies


def pages(pool, where, slots):
    return jnp.concatenate(
        [pool[pl.ds(pl.multiple_of(where[s], 16), PAGE), :] for s in slots], axis=0
    )


def score_kernel(count, n, table, krow, mark, lens, q, k_new, v_new, own_scales, *refs):
    keys, refs = refs[:n], refs[n:]
    weights, fresh_out, pool, ksc, vsc, score, sems = refs
    copies = load(keys, pool, sems)
    for copy in copies:
        copy.wait()
    for part in range(NZ):
        both = pool[pl.ds(part * PART + 2 * CODES, 16), :].astype(jnp.float32)
        ksc[pl.ds(part * EXPORT, EXPORT), :] = both[:EXPORT]
        vsc[pl.ds(part * EXPORT, EXPORT), :] = both[EXPORT:]
    for part in range(NX - 1):
        at = FAR + part * KPACK + TAKE * PAGE
        ksc[pl.ds(SFAR + part * TAKE, TAKE), :] = pool[pl.ds(at, TAKE), :].astype(jnp.float32)
        vsc[pl.ds(SFAR + part * TAKE, TAKE), :] = pool[pl.ds(at + TAKE, TAKE), :].astype(
            jnp.float32
        )
    mine = own_scales[...].astype(jnp.float32)
    ksc[pl.ds(SOWN, OWN), :] = mine[:OWN]
    vsc[pl.ds(SOWN, OWN), :] = mine[OWN:]

    rows = BLOCK * ROWS
    span = 4 * PAGE
    lane = lax.broadcasted_iota(jnp.int32, (1, HD), 1)
    token = lax.broadcasted_iota(jnp.int32, (ROWS, span), 1)

    def scale_row(ref, slots):
        pieces = []
        for m in range(0, len(slots), 2):
            left = ref[pl.ds(mark[slots[m]], 1), :]
            right = ref[pl.ds(mark[slots[m + 1]], 1), :]
            pieces.append(jnp.where(lane < PAGE, left, right))
        return jnp.concatenate(pieces, axis=1)

    def one_block(block, carry):
        base = block * BLOCK
        here = pl.ds(pl.multiple_of(block * rows, rows), rows)
        queries = q[here, :]
        for i in range(BLOCK):
            branch = base + i
            length = lens[branch]
            for half in range(2):
                slots = [table[branch * MAXP + half * 4 + m] for m in range(4)]
                s = lax.dot_general(
                    queries[i * ROWS : (i + 1) * ROWS],
                    pages(pool, krow, slots),
                    (((1,), (1,)), ((), ())),
                    preferred_element_type=jnp.float32,
                )
                live = token < length - half * span
                score[pl.ds(i * ROWS, ROWS), pl.ds(half * span, span)] = jnp.where(
                    live, s * scale_row(ksc, slots), NEG
                )
        new = pl.ds(pl.multiple_of(base * STEPS, BLOCK * STEPS), BLOCK * STEPS)
        fresh = lax.dot_general(
            queries, k_new[new, :], (((1,), (1,)), ((), ())), preferred_element_type=jnp.float32
        )
        row = lax.broadcasted_iota(jnp.int32, fresh.shape, 0)
        col = lax.broadcasted_iota(jnp.int32, fresh.shape, 1)
        step = lax.shift_right_logical(row, 2)
        same = lax.shift_right_logical(step, 2) == lax.shift_right_logical(col, 2)
        fresh = jnp.where(same & ((step & 3) >= (col & 3)), fresh, NEG)
        context = score[...]
        top = jnp.maximum(
            jnp.max(context, axis=1, keepdims=True), jnp.max(fresh, axis=1, keepdims=True)
        )
        context = jnp.exp(context - top)
        fresh = jnp.exp(fresh - top)
        total = jnp.sum(context, axis=1, keepdims=True) + jnp.sum(fresh, axis=1, keepdims=True)
        inverse = 1.0 / total
        score[...] = context * inverse
        fresh_out[here, :] = jnp.dot(
            (fresh * inverse).astype(jnp.bfloat16),
            v_new[new, :],
            preferred_element_type=jnp.float32,
        )
        for i in range(BLOCK):
            branch = base + i
            slots = [table[branch * MAXP + m] for m in range(MAXP)]
            there = pl.ds(pl.multiple_of(block * rows + i * ROWS, ROWS), ROWS)
            weights[there, :] = (
                score[pl.ds(i * ROWS, ROWS), :] * scale_row(vsc, slots)
            ).astype(jnp.bfloat16)
        return carry

    lax.fori_loop(0, count // BLOCK, one_block, 0)


def score(table, krow, mark, lens, q, k_new, v_new, own_scales, keys):
    count = lens.shape[0]
    krows = sum(k.shape[0] for k in keys)
    return pl.pallas_call(
        functools.partial(score_kernel, count, len(keys)),
        out_shape=(
            jax.ShapeDtypeStruct((count * ROWS, MAXP * PAGE), jnp.bfloat16),
            jax.ShapeDtypeStruct((count * ROWS, HD), jnp.float32),
        ),
        in_specs=[spec(pltpu.SMEM)] * 4 + [spec(pltpu.VMEM)] * 4 + [spec(pl.ANY)] * len(keys),
        out_specs=(spec(pltpu.VMEM),) * 2,
        scratch_shapes=[
            pltpu.VMEM((krows, HD), jnp.bfloat16),
            pltpu.VMEM((SOWN + OWN, HD), jnp.float32),
            pltpu.VMEM((SOWN + OWN, HD), jnp.float32),
            pltpu.VMEM((BLOCK * ROWS, MAXP * PAGE), jnp.float32),
            pltpu.SemaphoreType.DMA((len(keys),)),
        ],
        compiler_params=pltpu.CompilerParams(vmem_limit_bytes=LIMIT),
        name="score",
    )(table, krow, mark, lens, q, k_new, v_new, own_scales, *keys)


def value_kernel(first, count, n, table, vrow, weights, fresh, *refs):
    values, (out, pool, result, sems) = refs[:n], refs[n:]
    copies = load(values, pool, sems)
    for copy in copies:
        copy.wait()

    def one_block(block, carry):
        for i in range(BLOCK):
            branch = first + block * BLOCK + i
            slots = [table[branch * MAXP + m] for m in range(MAXP)]
            here = pl.ds(pl.multiple_of((block * BLOCK + i) * ROWS, ROWS), ROWS)
            part = jnp.dot(
                weights[here, :], pages(pool, vrow, slots), preferred_element_type=jnp.float32
            )
            result[here, :] = part + fresh[here, :]
        return carry

    lax.fori_loop(0, count // BLOCK, one_block, 0)
    for g in range(GROUP):
        out[:, g * HD : (g + 1) * HD] = result[
            pl.ds(g, count * STEPS, stride=GROUP), :
        ].astype(jnp.bfloat16)


def value(first, count, table, vrow, weights, fresh, values):
    vrows = sum(v.shape[0] for v in values)
    chunk = first // count
    return pl.pallas_call(
        functools.partial(value_kernel, first, count, len(values)),
        grid=(1,),
        out_shape=jax.ShapeDtypeStruct((count * STEPS, GROUP * HD), jnp.bfloat16),
        in_specs=[spec(pltpu.SMEM)] * 2
        + [
            pl.BlockSpec((count * ROWS, MAXP * PAGE), lambda i: (chunk, 0)),
            pl.BlockSpec((count * ROWS, HD), lambda i: (chunk, 0)),
        ]
        + [spec(pl.ANY)] * len(values),
        out_specs=spec(pltpu.VMEM),
        scratch_shapes=[
            pltpu.VMEM((vrows, HD), jnp.bfloat16),
            pltpu.VMEM((count * ROWS, HD), jnp.float32),
            pltpu.SemaphoreType.DMA((len(values),)),
        ],
        compiler_params=pltpu.CompilerParams(vmem_limit_bytes=LIMIT),
        name="value",
    )(table, vrow, weights, fresh, *values)


def mix_kernel(place, near, far, w_near, w_far, *outs):
    y, c = place[0], place[1]
    width = outs[0].shape[1]
    for j in (2, 1, 3, 0):
        at = pl.ds(pl.multiple_of((lax.rem(y + j, NY) * 2 + c) * width, width), width)
        total = jnp.dot(near[...], w_near[:, at], preferred_element_type=jnp.float32)
        total += jnp.dot(far[...], w_far[:, at], preferred_element_type=jnp.float32)
        outs[j][...] = total.astype(jnp.bfloat16)


def mix(place, near, far, w_near, w_far):
    tokens = near.shape[0]
    width = w_near.shape[1] // (2 * NY)
    out = jax.ShapeDtypeStruct((tokens, width), jnp.bfloat16)
    return pl.pallas_call(
        mix_kernel,
        out_shape=(out,) * NY,
        in_specs=[spec(pltpu.SMEM)] + [spec(pltpu.VMEM)] * 4,
        out_specs=(spec(pltpu.VMEM),) * NY,
        compiler_params=pltpu.CompilerParams(vmem_limit_bytes=LIMIT),
        name="mix",
    )(place, near, far, w_near, w_far)


def after(value, *others):
    return lax.optimization_barrier((value, *others))[0]


def plan_kernel(where, pull, rows, marks, krow, vrow, mark):
    z, x = where[0], where[1]

    def locate(j, side):
        name = pull[(z * NX + lax.rem(x + side, NX)) * FORK + j]
        source = lax.shift_right_logical(name, 3)
        dz = lax.shift_right_logical(source, 2) - z
        dx = (source & (NX - 1)) - x
        return name & (EXPORT - 1), dz & (NZ - 1), dx & (NX - 1)

    def clear(k, carry):
        rows[k] = 0
        marks[k] = 0
        return carry

    lax.fori_loop(0, (NX - 1) * TAKE, clear, 0, unroll=8)
    for side in range(1, NX):

        def send(j, count):
            entry, dz, dx = locate(j, side)
            match = dx == 0
            at = jnp.where(match, (side - 1) * TAKE + count, (NX - 1) * TAKE)
            rows[at] = dz * PART + entry * PAGE
            marks[at] = dz * EXPORT + entry
            return count + match.astype(jnp.int32)

        lax.fori_loop(0, FORK, send, 0, unroll=8)

    def take(j, counts):
        entry, dz, dx = locate(j, 0)
        rank = jnp.where(dx == 1, counts[0], jnp.where(dx == 2, counts[1], counts[2]))
        near = dx == 0
        krow[j] = jnp.where(
            near, dz * PART + entry * PAGE, FAR + (dx - 1) * KPACK + rank * PAGE
        )
        mark[j] = jnp.where(near, dz * EXPORT + entry, SFAR + (dx - 1) * TAKE + rank)
        vrow[j] = jnp.where(
            near, dz * PART + CODES + entry * PAGE, FAR + (dx - 1) * VPACK + rank * PAGE
        )
        return tuple(counts[k] + (dx == k + 1).astype(jnp.int32) for k in range(NX - 1))

    zero = jnp.int32(0)
    lax.fori_loop(0, FORK, take, (zero,) * (NX - 1), unroll=8)

    def own(i, carry):
        krow[FORK + i] = KOWN + i * PAGE
        vrow[FORK + i] = VOWN + i * PAGE
        mark[FORK + i] = SOWN + i
        return carry

    lax.fori_loop(0, OWN, own, 0, unroll=8)


def plan(where, fork_pull):
    sends = jax.ShapeDtypeStruct(((NX - 1) * TAKE + 1,), jnp.int32)
    slots = jax.ShapeDtypeStruct((FORK + OWN,), jnp.int32)
    return pl.pallas_call(
        plan_kernel,
        out_shape=(sends, sends, slots, slots, slots),
        in_specs=[spec(pltpu.SMEM)] * 2,
        out_specs=(spec(pltpu.SMEM),) * 5,
        name="plan",
    )(where, fork_pull.reshape(-1))


def per_device(
    hidden,
    gain,
    w_query,
    w_keyval,
    w_out,
    kv_codes,
    kv_scales,
    fork_export,
    fork_pull,
    page_table,
    lengths,
):
    branches, steps, width = hidden.shape
    rows = branches * steps
    tensor = lax.axis_index("tensor")
    myself = lax.axis_index("branch")
    place = jnp.stack([tensor // 2, tensor % 2]).astype(jnp.int32)

    where = jnp.stack([myself // NX, myself % NX]).astype(jnp.int32)
    flat_scales = kv_scales.astype(jnp.float32).reshape(-1)
    part = export_pages(kv_codes, flat_scales, fork_export)
    own = after(hidden.reshape(rows, width), part)
    z = {0: part, 1: from_z(part, 1, "pages1"), -1: from_z(part, -1, "pages1")}
    aside = [from_y(own, d, "hidden") for d in (1, 2, 3)]
    w_far = from_core(w_out, "w_out")
    own_far = from_core(own, "hidden_core")
    z[2] = from_z(after(z[1], own_far, w_far), 1, "pages2")
    z[-2] = from_z(after(z[-1], own_far, w_far), -1, "pages2")
    where = after(where, z[1], z[-1])
    send_rows, send_marks, krow, vrow, mark = plan(where, fork_pull)
    z[2], z[-2] = after(z[2], send_rows), after(z[-2], send_rows)
    z[3], z[-3] = from_z(z[2], 1, "pages3"), from_z(z[-2], -1, "pages3")
    z[4] = from_z(after(z[3], z[-3]), 1, "pages4")
    parts = [own, *aside, own_far]
    parts += [from_core(after(part, z[2], z[-2]), "hidden_core") for part in aside]
    column = [z[d] for d in (0, 1, 2, 3, 4, -3, -2, -1)]
    column[0] = after(column[0], *parts)

    def sides(plus, across, minus, name):
        return [from_x(minus, 1, name), from_x(across, 2, name), from_x(plus, -1, name)]

    packed = pack(0, send_rows, send_marks, column)
    keys = column + sides(*packed, "key_side")

    half = HD // 2
    freq = jnp.exp(-(2.0 * jnp.arange(half).astype(jnp.float32) / HD) * math.log(500000.0))
    positions = (lengths[:, None] + jnp.arange(steps, dtype=jnp.int32)[None, :]).reshape(-1)
    angle = positions.astype(jnp.float32)[:, None] * freq[None, :]
    cos, sin = jnp.cos(angle), jnp.sin(angle)
    cosine = jnp.concatenate([cos, cos], axis=1)
    sine = jnp.concatenate([-sin, sin], axis=1)
    q, k_new, v_new = project(
        place, parts, gain.reshape(2 * NY, width), w_query, w_keyval, cosine, sine
    )

    keys = keys + [kv_codes[:, 0].reshape(OWN * PAGE, HD)]
    own_scales = jnp.broadcast_to(
        jnp.transpose(kv_scales, (1, 0, 2)).reshape(2 * OWN, 1), (2 * OWN, HD)
    )
    table = page_table.reshape(-1)

    column[0] = after(column[0], q)
    plus, across, minus = pack(1, send_rows, send_marks, column)
    values = column + sides(plus, across, minus, "value_side")
    values = values + [kv_codes[:, 1].reshape(OWN * PAGE, HD)]
    weights, fresh = score(table, krow, mark, lengths, q, k_new, v_new, own_scales, keys)
    attended = value(0, branches, table, vrow, weights, fresh, values)
    other = from_core(attended, "attended_core")
    total, plus, across, minus = mix(place, attended, other, w_out, w_far)
    got = [
        from_y(across, -2, "output"),
        from_y(plus, -1, "output"),
        from_y(minus, -3, "output"),
    ]
    total = total.astype(jnp.float32)
    for piece in got:
        total = total + piece.astype(jnp.float32)
    return total.astype(jnp.bfloat16).reshape(branches, steps, width)


def solution(mesh):
    return jax.shard_map(
        per_device,
        mesh=mesh,
        in_specs=(
            P("branch", None, "tensor"),
            P(),
            P(None, "tensor"),
            P(None, None, "tensor"),
            P("tensor", None),
            P("branch", None, None, "tensor"),
            P("branch", None, "tensor"),
            P("branch"),
            P(),
            P("branch", None),
            P("branch"),
        ),
        out_specs=P("branch", None, "tensor"),
        check_vma=False,
    )
```

```python
import functools
import math

import jax
import jax.numpy as jnp
from jax import lax
from jax.experimental import pallas as pl
from jax.experimental.pallas import tpu as pltpu
from jax.sharding import PartitionSpec as P

HEADS = 32
KVH = 8
HD = 128
PAGE = 64
MAXP = 8
STEPS = 4
GROUP = HEADS // KVH
OWN = 32
FORK = 64
EXPORT = 8
NZ, NX, NY = 8, 4, 4
ROWS = GROUP * STEPS
CODES = EXPORT * PAGE
PART = 2 * CODES + 16
TAKE = NZ * 4
FAR = NZ * PART
KPACK = TAKE * PAGE + 2 * TAKE
VPACK = TAKE * PAGE
KOWN = FAR + (NX - 1) * KPACK
VOWN = FAR + (NX - 1) * VPACK
SFAR = NZ * EXPORT
SOWN = SFAR + (NX - 1) * TAKE
BLOCK = 16
NEG = -1e30
LIMIT = 30 * 1024 * 1024


def from_z(value, d, name="z"):
    perm = [(z * NX + x, ((z - d) % NZ) * NX + x) for z in range(NZ) for x in range(NX)]
    with jax.named_scope(name):
        return lax.ppermute(value, "branch", perm)


def from_x(value, d, name="x"):
    perm = [(z * NX + x, z * NX + (x - d) % NX) for z in range(NZ) for x in range(NX)]
    with jax.named_scope(name):
        return lax.ppermute(value, "branch", perm)


def from_y(value, d, name="y"):
    perm = [(y * 2 + c, ((y - d) % NY) * 2 + c) for y in range(NY) for c in range(2)]
    with jax.named_scope(name):
        return lax.ppermute(value, "tensor", perm)


def from_core(value, name="core"):
    with jax.named_scope(name):
        return lax.ppermute(value, "tensor", [(t, t ^ 1) for t in range(2 * NY)])


def spec(space):
    return pl.BlockSpec(memory_space=space)


def export_kernel(picks, scales, codes, out, sems):
    copies = []
    for e in range(EXPORT):
        page = picks[e]
        for kind in range(2):
            rows = pl.ds(kind * CODES + e * PAGE, PAGE)
            copies.append(
                pltpu.make_async_copy(codes.at[page, kind], out.at[rows, :], sems.at[2 * e + kind])
            )
            copies[-1].start()
    place = lax.broadcasted_iota(jnp.int32, (16, HD), 0)
    rows = jnp.zeros((16, HD), jnp.float32)
    table = scales[...].astype(jnp.float32)
    lane = lax.broadcasted_iota(jnp.int32, table.shape, 1)
    for e in range(EXPORT):
        pair = jnp.sum(jnp.where(lane == picks[e], table, 0.0), axis=1, keepdims=True)
        for kind in range(2):
            rows = jnp.where(place == kind * EXPORT + e, pair[kind : kind + 1, :], rows)
    out[pl.ds(2 * CODES, 16), :] = rows.astype(jnp.bfloat16)
    for copy in copies:
        copy.wait()


def export_pages(codes, scales, picks):
    return pl.pallas_call(
        export_kernel,
        out_shape=jax.ShapeDtypeStruct((PART, HD), jnp.bfloat16),
        in_specs=[spec(pltpu.SMEM), spec(pltpu.VMEM), spec(pl.ANY)],
        out_specs=spec(pltpu.VMEM),
        scratch_shapes=[pltpu.SemaphoreType.DMA((2 * EXPORT,))],
        name="export_pages",
    )(picks, scales, codes)


def pack_kernel(kind, rows, marks, *refs):
    parts, outs = refs[:NZ], refs[NZ : NZ + NX - 1]
    pool, both, ksc, vsc, kout, vout, sems = refs[NZ + NX - 1 :]
    copies = []
    for i, part in enumerate(parts):
        ends = ((part, kind * CODES, pool, CODES), (part, 2 * CODES, both, 16))
        for source, at, target, n in ends[: 2 - kind]:
            to = target.at[pl.ds(i * n, n), :]
            sem = sems.at[2 * i + (target is both)]
            copies.append(pltpu.make_async_copy(source.at[pl.ds(at, n), :], to, sem))
            copies[-1].start()
    for copy in copies:
        copy.wait()
    if kind == 0:
        for i in range(NZ):
            pair = both[pl.ds(i * 16, 16), :].astype(jnp.float32)
            ksc[pl.ds(i * EXPORT, EXPORT), :] = pair[:EXPORT]
            vsc[pl.ds(i * EXPORT, EXPORT), :] = pair[EXPORT:]
    for d, out in enumerate(outs):
        for k in range(TAKE):
            row = pl.multiple_of(rows[d * TAKE + k], 16)
            out[pl.ds(k * PAGE, PAGE), :] = pool[pl.ds(row, PAGE), :]
        if kind == 0:
            for k in range(TAKE):
                mark = marks[d * TAKE + k]
                kout[pl.ds(k, 1), :] = ksc[pl.ds(mark, 1), :]
                vout[pl.ds(k, 1), :] = vsc[pl.ds(mark, 1), :]
            out[pl.ds(TAKE * PAGE, TAKE), :] = kout[...].astype(jnp.bfloat16)
            out[pl.ds(TAKE * PAGE + TAKE, TAKE), :] = vout[...].astype(jnp.bfloat16)


def pack(kind, rows, marks, parts):
    out = jax.ShapeDtypeStruct((VPACK if kind else KPACK, HD), jnp.bfloat16)
    return pl.pallas_call(
        functools.partial(pack_kernel, kind),
        out_shape=(out,) * (NX - 1),
        in_specs=[spec(pltpu.SMEM)] * 2 + [spec(pl.ANY)] * NZ,
        out_specs=(spec(pltpu.VMEM),) * (NX - 1),
        scratch_shapes=[
            pltpu.VMEM((NZ * CODES, HD), jnp.bfloat16),
            pltpu.VMEM((NZ * 16, HD), jnp.bfloat16),
            pltpu.VMEM((SFAR, HD), jnp.float32),
            pltpu.VMEM((SFAR, HD), jnp.float32),
            pltpu.VMEM((TAKE, HD), jnp.float32),
            pltpu.VMEM((TAKE, HD), jnp.float32),
            pltpu.SemaphoreType.DMA((2 * NZ,)),
        ],
        name="pack",
    )(rows, marks, *parts)


def project_kernel(place, *refs):
    parts = refs[:8]
    gain, w_query, w_keyval, cosine, sine, q_out, k_out, v_out, qf = refs[8:]
    y, c = place[0], place[1]
    rows = parts[0].shape[0]
    width = parts[0].shape[1]
    power = jnp.zeros((rows, 1), jnp.float32)
    acc_q = jnp.zeros((rows, GROUP * HD), jnp.float32)
    acc_k = jnp.zeros((rows, HD), jnp.float32)
    acc_v = jnp.zeros((rows, HD), jnp.float32)
    for index, part in enumerate(parts):
        core = c if index < NY else 1 - c
        t = lax.rem(y + index % NY, NY) * 2 + core
        feats = part[...].astype(jnp.float32)
        power = power + jnp.sum(feats * feats, axis=1, keepdims=True)
        scaled = (feats * gain[pl.ds(t, 1), :]).astype(jnp.bfloat16)
        here = pl.ds(pl.multiple_of(t * width, width), width)
        acc_q = acc_q + jnp.dot(scaled, w_query[here, :], preferred_element_type=jnp.float32)
        acc_k = acc_k + jnp.dot(scaled, w_keyval[0, here, :], preferred_element_type=jnp.float32)
        acc_v = acc_v + jnp.dot(scaled, w_keyval[1, here, :], preferred_element_type=jnp.float32)
    norm = lax.rsqrt(power / (width * 8) + 1e-05)
    cos, sin = cosine[...], sine[...]

    def rope(v):
        return v * cos + pltpu.roll(v, HD // 2, 1) * sin

    for g in range(GROUP):
        head = rope(acc_q[:, g * HD : (g + 1) * HD] * norm) * HD ** (-0.5)
        qf[pl.ds(g, rows, stride=GROUP), :] = head
    q_out[...] = qf[...].astype(jnp.bfloat16)
    k_out[...] = rope(acc_k * norm).astype(jnp.bfloat16)
    v_out[...] = (acc_v * norm).astype(jnp.bfloat16)


def project(place, parts, gain, w_query, w_keyval, cosine, sine):
    rows = parts[0].shape[0]
    return pl.pallas_call(
        project_kernel,
        out_shape=(
            jax.ShapeDtypeStruct((rows * GROUP, HD), jnp.bfloat16),
            jax.ShapeDtypeStruct((rows, HD), jnp.bfloat16),
            jax.ShapeDtypeStruct((rows, HD), jnp.bfloat16),
        ),
        in_specs=[spec(pltpu.SMEM)] + [spec(pltpu.VMEM)] * 13,
        out_specs=(spec(pltpu.VMEM),) * 3,
        scratch_shapes=[pltpu.VMEM((rows * GROUP, HD), jnp.float32)],
        compiler_params=pltpu.CompilerParams(vmem_limit_bytes=LIMIT),
        name="project",
    )(place, *parts, gain, w_query, w_keyval, cosine, sine)


def load(parts, pool, sems):
    copies, at = [], 0
    for i, part in enumerate(parts):
        n = part.shape[0]
        copies.append(pltpu.make_async_copy(part, pool.at[pl.ds(at, n), :], sems.at[i]))
        copies[-1].start()
        at += n
    return copies


def pages(pool, where, slots):
    return jnp.concatenate(
        [pool[pl.ds(pl.multiple_of(where[s], 16), PAGE), :] for s in slots], axis=0
    )


def score_kernel(count, n, table, krow, mark, lens, q, k_new, v_new, own_scales, *refs):
    keys, refs = refs[:n], refs[n:]
    weights, fresh_out, pool, ksc, vsc, score, sems = refs
    copies = load(keys, pool, sems)
    for copy in copies:
        copy.wait()
    for part in range(NZ):
        both = pool[pl.ds(part * PART + 2 * CODES, 16), :].astype(jnp.float32)
        ksc[pl.ds(part * EXPORT, EXPORT), :] = both[:EXPORT]
        vsc[pl.ds(part * EXPORT, EXPORT), :] = both[EXPORT:]
    for part in range(NX - 1):
        at = FAR + part * KPACK + TAKE * PAGE
        ksc[pl.ds(SFAR + part * TAKE, TAKE), :] = pool[pl.ds(at, TAKE), :].astype(jnp.float32)
        vsc[pl.ds(SFAR + part * TAKE, TAKE), :] = pool[pl.ds(at + TAKE, TAKE), :].astype(
            jnp.float32
        )
    mine = own_scales[...].astype(jnp.float32)
    ksc[pl.ds(SOWN, OWN), :] = mine[:OWN]
    vsc[pl.ds(SOWN, OWN), :] = mine[OWN:]

    rows = BLOCK * ROWS
    span = 4 * PAGE
    lane = lax.broadcasted_iota(jnp.int32, (1, HD), 1)
    token = lax.broadcasted_iota(jnp.int32, (ROWS, span), 1)

    def scale_row(ref, slots):
        pieces = []
        for m in range(0, len(slots), 2):
            left = ref[pl.ds(mark[slots[m]], 1), :]
            right = ref[pl.ds(mark[slots[m + 1]], 1), :]
            pieces.append(jnp.where(lane < PAGE, left, right))
        return jnp.concatenate(pieces, axis=1)

    def one_block(block, carry):
        base = block * BLOCK
        here = pl.ds(pl.multiple_of(block * rows, rows), rows)
        queries = q[here, :]
        for i in range(BLOCK):
            branch = base + i
            length = lens[branch]
            for half in range(2):
                slots = [table[branch * MAXP + half * 4 + m] for m in range(4)]
                s = lax.dot_general(
                    queries[i * ROWS : (i + 1) * ROWS],
                    pages(pool, krow, slots),
                    (((1,), (1,)), ((), ())),
                    preferred_element_type=jnp.float32,
                )
                live = token < length - half * span
                score[pl.ds(i * ROWS, ROWS), pl.ds(half * span, span)] = jnp.where(
                    live, s * scale_row(ksc, slots), NEG
                )
        new = pl.ds(pl.multiple_of(base * STEPS, BLOCK * STEPS), BLOCK * STEPS)
        fresh = lax.dot_general(
            queries, k_new[new, :], (((1,), (1,)), ((), ())), preferred_element_type=jnp.float32
        )
        row = lax.broadcasted_iota(jnp.int32, fresh.shape, 0)
        col = lax.broadcasted_iota(jnp.int32, fresh.shape, 1)
        step = lax.shift_right_logical(row, 2)
        same = lax.shift_right_logical(step, 2) == lax.shift_right_logical(col, 2)
        fresh = jnp.where(same & ((step & 3) >= (col & 3)), fresh, NEG)
        context = score[...]
        top = jnp.maximum(
            jnp.max(context, axis=1, keepdims=True), jnp.max(fresh, axis=1, keepdims=True)
        )
        context = jnp.exp(context - top)
        fresh = jnp.exp(fresh - top)
        total = jnp.sum(context, axis=1, keepdims=True) + jnp.sum(fresh, axis=1, keepdims=True)
        inverse = 1.0 / total
        score[...] = context * inverse
        fresh_out[here, :] = jnp.dot(
            (fresh * inverse).astype(jnp.bfloat16),
            v_new[new, :],
            preferred_element_type=jnp.float32,
        )
        for i in range(BLOCK):
            branch = base + i
            slots = [table[branch * MAXP + m] for m in range(MAXP)]
            there = pl.ds(pl.multiple_of(block * rows + i * ROWS, ROWS), ROWS)
            weights[there, :] = (
                score[pl.ds(i * ROWS, ROWS), :] * scale_row(vsc, slots)
            ).astype(jnp.bfloat16)
        return carry

    lax.fori_loop(0, count // BLOCK, one_block, 0)


def score(table, krow, mark, lens, q, k_new, v_new, own_scales, keys):
    count = lens.shape[0]
    krows = sum(k.shape[0] for k in keys)
    return pl.pallas_call(
        functools.partial(score_kernel, count, len(keys)),
        out_shape=(
            jax.ShapeDtypeStruct((count * ROWS, MAXP * PAGE), jnp.bfloat16),
            jax.ShapeDtypeStruct((count * ROWS, HD), jnp.float32),
        ),
        in_specs=[spec(pltpu.SMEM)] * 4 + [spec(pltpu.VMEM)] * 4 + [spec(pl.ANY)] * len(keys),
        out_specs=(spec(pltpu.VMEM),) * 2,
        scratch_shapes=[
            pltpu.VMEM((krows, HD), jnp.bfloat16),
            pltpu.VMEM((SOWN + OWN, HD), jnp.float32),
            pltpu.VMEM((SOWN + OWN, HD), jnp.float32),
            pltpu.VMEM((BLOCK * ROWS, MAXP * PAGE), jnp.float32),
            pltpu.SemaphoreType.DMA((len(keys),)),
        ],
        compiler_params=pltpu.CompilerParams(vmem_limit_bytes=LIMIT),
        name="score",
    )(table, krow, mark, lens, q, k_new, v_new, own_scales, *keys)


def value_kernel(first, count, n, table, vrow, weights, fresh, *refs):
    values, (out, pool, result, sems) = refs[:n], refs[n:]
    copies = load(values, pool, sems)
    for copy in copies:
        copy.wait()

    def one_block(block, carry):
        for i in range(BLOCK):
            branch = first + block * BLOCK + i
            slots = [table[branch * MAXP + m] for m in range(MAXP)]
            here = pl.ds(pl.multiple_of((block * BLOCK + i) * ROWS, ROWS), ROWS)
            part = jnp.dot(
                weights[here, :], pages(pool, vrow, slots), preferred_element_type=jnp.float32
            )
            result[here, :] = part + fresh[here, :]
        return carry

    lax.fori_loop(0, count // BLOCK, one_block, 0)
    for g in range(GROUP):
        out[:, g * HD : (g + 1) * HD] = result[
            pl.ds(g, count * STEPS, stride=GROUP), :
        ].astype(jnp.bfloat16)


def value(first, count, table, vrow, weights, fresh, values):
    vrows = sum(v.shape[0] for v in values)
    chunk = first // count
    return pl.pallas_call(
        functools.partial(value_kernel, first, count, len(values)),
        grid=(1,),
        out_shape=jax.ShapeDtypeStruct((count * STEPS, GROUP * HD), jnp.bfloat16),
        in_specs=[spec(pltpu.SMEM)] * 2
        + [
            pl.BlockSpec((count * ROWS, MAXP * PAGE), lambda i: (chunk, 0)),
            pl.BlockSpec((count * ROWS, HD), lambda i: (chunk, 0)),
        ]
        + [spec(pl.ANY)] * len(values),
        out_specs=spec(pltpu.VMEM),
        scratch_shapes=[
            pltpu.VMEM((vrows, HD), jnp.bfloat16),
            pltpu.VMEM((count * ROWS, HD), jnp.float32),
            pltpu.SemaphoreType.DMA((len(values),)),
        ],
        compiler_params=pltpu.CompilerParams(vmem_limit_bytes=LIMIT),
        name="value",
    )(table, vrow, weights, fresh, *values)


def mix_kernel(blocks, place, near, far, w_near, w_far, *outs):
    y, c = place[0], place[1]
    width = outs[0].shape[1]
    for j, out in zip(blocks, outs):
        at = pl.ds(pl.multiple_of((lax.rem(y + j, NY) * 2 + c) * width, width), width)
        total = jnp.dot(near[...], w_near[:, at], preferred_element_type=jnp.float32)
        total += jnp.dot(far[...], w_far[:, at], preferred_element_type=jnp.float32)
        out[...] = total.astype(jnp.bfloat16)


def mix(blocks, place, near, far, w_near, w_far):
    tokens = near.shape[0]
    width = w_near.shape[1] // (2 * NY)
    out = jax.ShapeDtypeStruct((tokens, width), jnp.bfloat16)
    return pl.pallas_call(
        functools.partial(mix_kernel, blocks),
        out_shape=(out,) * len(blocks),
        in_specs=[spec(pltpu.SMEM)] + [spec(pltpu.VMEM)] * 4,
        out_specs=(spec(pltpu.VMEM),) * len(blocks),
        compiler_params=pltpu.CompilerParams(vmem_limit_bytes=LIMIT),
        name="mix",
    )(place, near, far, w_near, w_far)


def after(value, *others):
    return lax.optimization_barrier((value, *others))[0]


def plan_kernel(where, pull, rows, marks, krow, vrow, mark):
    z, x = where[0], where[1]

    def locate(j, side):
        name = pull[(z * NX + lax.rem(x + side, NX)) * FORK + j]
        source = lax.shift_right_logical(name, 3)
        dz = lax.shift_right_logical(source, 2) - z
        dx = (source & (NX - 1)) - x
        return name & (EXPORT - 1), dz & (NZ - 1), dx & (NX - 1)

    def clear(k, carry):
        rows[k] = 0
        marks[k] = 0
        return carry

    lax.fori_loop(0, (NX - 1) * TAKE, clear, 0, unroll=8)
    for side in range(1, NX):

        def send(j, count):
            entry, dz, dx = locate(j, side)
            match = dx == 0
            at = jnp.where(match, (side - 1) * TAKE + count, (NX - 1) * TAKE)
            rows[at] = dz * CODES + entry * PAGE
            marks[at] = dz * EXPORT + entry
            return count + match.astype(jnp.int32)

        lax.fori_loop(0, FORK, send, 0, unroll=8)

    def take(j, counts):
        entry, dz, dx = locate(j, 0)
        rank = jnp.where(dx == 1, counts[0], jnp.where(dx == 2, counts[1], counts[2]))
        near = dx == 0
        krow[j] = jnp.where(
            near, dz * PART + entry * PAGE, FAR + (dx - 1) * KPACK + rank * PAGE
        )
        mark[j] = jnp.where(near, dz * EXPORT + entry, SFAR + (dx - 1) * TAKE + rank)
        vrow[j] = jnp.where(
            near, dz * PART + CODES + entry * PAGE, FAR + (dx - 1) * VPACK + rank * PAGE
        )
        return tuple(counts[k] + (dx == k + 1).astype(jnp.int32) for k in range(NX - 1))

    zero = jnp.int32(0)
    lax.fori_loop(0, FORK, take, (zero,) * (NX - 1), unroll=8)

    def own(i, carry):
        krow[FORK + i] = KOWN + i * PAGE
        vrow[FORK + i] = VOWN + i * PAGE
        mark[FORK + i] = SOWN + i
        return carry

    lax.fori_loop(0, OWN, own, 0, unroll=8)


def plan(where, fork_pull):
    sends = jax.ShapeDtypeStruct(((NX - 1) * TAKE + 1,), jnp.int32)
    slots = jax.ShapeDtypeStruct((FORK + OWN,), jnp.int32)
    return pl.pallas_call(
        plan_kernel,
        out_shape=(sends, sends, slots, slots, slots),
        in_specs=[spec(pltpu.SMEM)] * 2,
        out_specs=(spec(pltpu.SMEM),) * 5,
        name="plan",
    )(where, fork_pull.reshape(-1))


def per_device(
    hidden,
    gain,
    w_query,
    w_keyval,
    w_out,
    kv_codes,
    kv_scales,
    fork_export,
    fork_pull,
    page_table,
    lengths,
):
    branches, steps, width = hidden.shape
    rows = branches * steps
    tensor = lax.axis_index("tensor")
    myself = lax.axis_index("branch")
    place = jnp.stack([tensor // 2, tensor % 2]).astype(jnp.int32)

    where = jnp.stack([myself // NX, myself % NX]).astype(jnp.int32)
    part = export_pages(kv_codes, kv_scales.transpose(2, 1, 0).reshape(2, OWN), fork_export)
    own = after(hidden, part).reshape(rows, width)
    z = {0: part, 1: from_z(part, 1, "pages1"), -1: from_z(part, -1, "pages1")}
    aside = [from_y(own, d, "hidden") for d in (1, 2, 3)]
    w_far = from_core(w_out, "w_out")
    own_far = from_core(own, "hidden_core")
    z[2] = from_z(after(z[1], own_far, w_far), 1, "pages2")
    z[-2] = from_z(after(z[-1], own_far, w_far), -1, "pages2")
    half = HD // 2
    freq = jnp.exp(-(2.0 * jnp.arange(half).astype(jnp.float32) / HD) * math.log(500000.0))
    positions = (after(lengths, z[1], z[-1])[:, None] + jnp.arange(steps, dtype=jnp.int32)[None, :]).reshape(-1)
    angle = positions.astype(jnp.float32)[:, None] * freq[None, :]
    cos, sin = jnp.cos(angle), jnp.sin(angle)
    cosine = jnp.concatenate([cos, cos], axis=1)
    sine = jnp.concatenate([-sin, sin], axis=1)
    z[2], z[-2] = after(z[2], cosine, sine), after(z[-2], cosine, sine)
    z[3], z[-3] = from_z(z[2], 1, "pages3"), from_z(z[-2], -1, "pages3")
    z[4] = from_z(after(z[3], z[-3]), 1, "pages4")
    where = after(where, z[3], z[-3])
    send_rows, send_marks, krow, vrow, mark = plan(where, fork_pull)
    plus_far, across_far = [
        from_core(after(aside[i], z[2], z[-2]), "hidden_core") for i in (0, 1)
    ]
    column = [z[d] for d in (0, 1, 2, 3, 4, -3, -2, -1)]
    column[0] = after(column[0], plus_far, across_far)

    def sides(plus, across, minus, name):
        return [from_x(minus, 1, name), from_x(across, 2, name), from_x(plus, -1, name)]

    packed = pack(0, send_rows, send_marks, column)
    keys = column + sides(*packed, "key_side")
    minus_far = from_core(after(aside[2], *packed), "hidden_core")
    column[0] = after(column[0], *packed, minus_far)
    plus, across, minus = pack(1, send_rows, send_marks, column)
    parts = [own, *aside, own_far, plus_far, across_far, minus_far]

    q, k_new, v_new = project(
        place, parts, gain.reshape(2 * NY, width), w_query, w_keyval, cosine, sine
    )

    keys = keys + [kv_codes[:, 0].reshape(OWN * PAGE, HD)]
    own_scales = jnp.broadcast_to(
        jnp.transpose(kv_scales, (1, 0, 2)).reshape(2 * OWN, 1), (2 * OWN, HD)
    )
    table = page_table.reshape(-1)

    across = after(across, q)
    values = column + sides(plus, across, minus, "value_side")
    values = values + [kv_codes[:, 1].reshape(OWN * PAGE, HD)]
    weights, fresh = score(table, krow, mark, lengths, q, k_new, v_new, own_scales, keys)
    attended = value(0, branches, table, vrow, weights, fresh, values)
    other = from_core(attended, "attended_core")
    (across,) = mix((2,), place, attended, other, w_out, w_far)
    got = [from_y(across, 2, "output_across")]
    attended = after(attended, across)
    total, plus, minus = mix((0, 1, 3), place, attended, other, w_out, w_far)
    got += [from_y(plus, -1, "output"), from_y(minus, 1, "output")]
    total = total.astype(jnp.float32)
    for piece in got:
        total = total + piece.astype(jnp.float32)
    return total.astype(jnp.bfloat16).reshape(branches, steps, width)


def solution(mesh):
    return jax.shard_map(
        per_device,
        mesh=mesh,
        in_specs=(
            P("branch", None, "tensor"),
            P(),
            P(None, "tensor"),
            P(None, None, "tensor"),
            P("tensor", None),
            P("branch", None, None, "tensor"),
            P("branch", None, "tensor"),
            P("branch"),
            P(),
            P("branch", None),
            P("branch"),
        ),
        out_specs=P("branch", None, "tensor"),
        check_vma=False,
    )
```

```python
import functools
import math

import jax
import jax.numpy as jnp
from jax import lax
from jax.experimental import pallas as pl
from jax.experimental.pallas import tpu as pltpu
from jax.sharding import PartitionSpec as P

HEADS = 32
KVH = 8
HD = 128
PAGE = 64
MAXP = 8
STEPS = 4
GROUP = HEADS // KVH
OWN = 32
FORK = 64
EXPORT = 8
NZ, NX, NY = 8, 4, 4
ROWS = GROUP * STEPS
CODES = EXPORT * PAGE
PART = 2 * CODES + 16
TAKE = NZ * 4
FAR = NZ * PART
KPACK = TAKE * PAGE + 2 * TAKE
VPACK = TAKE * PAGE
KOWN = FAR + (NX - 1) * KPACK
VOWN = FAR + (NX - 1) * VPACK
SFAR = NZ * EXPORT
SOWN = SFAR + (NX - 1) * TAKE
BLOCK = 16
NEG = -1e30
LIMIT = 30 * 1024 * 1024


def from_z(value, d, name="z"):
    perm = [(z * NX + x, ((z - d) % NZ) * NX + x) for z in range(NZ) for x in range(NX)]
    with jax.named_scope(name):
        return lax.ppermute(value, "branch", perm)


def from_x(value, d, name="x"):
    perm = [(z * NX + x, z * NX + (x - d) % NX) for z in range(NZ) for x in range(NX)]
    with jax.named_scope(name):
        return lax.ppermute(value, "branch", perm)


def from_y(value, d, name="y"):
    perm = [(y * 2 + c, ((y - d) % NY) * 2 + c) for y in range(NY) for c in range(2)]
    with jax.named_scope(name):
        return lax.ppermute(value, "tensor", perm)


def from_core(value, name="core"):
    with jax.named_scope(name):
        return lax.ppermute(value, "tensor", [(t, t ^ 1) for t in range(2 * NY)])


def spec(space):
    return pl.BlockSpec(memory_space=space)


def export_kernel(picks, scales, codes, out, sems):
    copies = []
    for e in range(EXPORT):
        page = picks[e]
        for kind in range(2):
            rows = pl.ds(kind * CODES + e * PAGE, PAGE)
            copies.append(
                pltpu.make_async_copy(codes.at[page, kind], out.at[rows, :], sems.at[2 * e + kind])
            )
            copies[-1].start()
    place = lax.broadcasted_iota(jnp.int32, (16, HD), 0)
    rows = jnp.zeros((16, HD), jnp.float32)
    table = scales[...].astype(jnp.float32)
    lane = lax.broadcasted_iota(jnp.int32, table.shape, 1)
    for e in range(EXPORT):
        pair = jnp.sum(jnp.where(lane == picks[e], table, 0.0), axis=1, keepdims=True)
        for kind in range(2):
            rows = jnp.where(place == kind * EXPORT + e, pair[kind : kind + 1, :], rows)
    out[pl.ds(2 * CODES, 16), :] = rows.astype(jnp.bfloat16)
    for copy in copies:
        copy.wait()


def export_pages(codes, scales, picks):
    return pl.pallas_call(
        export_kernel,
        out_shape=jax.ShapeDtypeStruct((PART, HD), jnp.bfloat16),
        in_specs=[spec(pltpu.SMEM), spec(pltpu.VMEM), spec(pl.ANY)],
        out_specs=spec(pltpu.VMEM),
        scratch_shapes=[pltpu.SemaphoreType.DMA((2 * EXPORT,))],
        name="export_pages",
    )(picks, scales, codes)


def pack_kernel(kind, rows, marks, *refs):
    parts, outs = refs[:NZ], refs[NZ : NZ + NX - 1]
    pool, both, ksc, vsc, kout, vout, sems = refs[NZ + NX - 1 :]
    copies = []
    for i, part in enumerate(parts):
        ends = ((part, kind * CODES, pool, CODES), (part, 2 * CODES, both, 16))
        for source, at, target, n in ends[: 2 - kind]:
            to = target.at[pl.ds(i * n, n), :]
            sem = sems.at[2 * i + (target is both)]
            copies.append(pltpu.make_async_copy(source.at[pl.ds(at, n), :], to, sem))
            copies[-1].start()
    for copy in copies:
        copy.wait()
    if kind == 0:
        for i in range(NZ):
            pair = both[pl.ds(i * 16, 16), :].astype(jnp.float32)
            ksc[pl.ds(i * EXPORT, EXPORT), :] = pair[:EXPORT]
            vsc[pl.ds(i * EXPORT, EXPORT), :] = pair[EXPORT:]
    for d, out in enumerate(outs):
        for k in range(TAKE):
            row = pl.multiple_of(rows[d * TAKE + k], 16)
            out[pl.ds(k * PAGE, PAGE), :] = pool[pl.ds(row, PAGE), :]
        if kind == 0:
            for k in range(TAKE):
                mark = marks[d * TAKE + k]
                kout[pl.ds(k, 1), :] = ksc[pl.ds(mark, 1), :]
                vout[pl.ds(k, 1), :] = vsc[pl.ds(mark, 1), :]
            out[pl.ds(TAKE * PAGE, TAKE), :] = kout[...].astype(jnp.bfloat16)
            out[pl.ds(TAKE * PAGE + TAKE, TAKE), :] = vout[...].astype(jnp.bfloat16)


def pack(kind, rows, marks, parts):
    out = jax.ShapeDtypeStruct((VPACK if kind else KPACK, HD), jnp.bfloat16)
    return pl.pallas_call(
        functools.partial(pack_kernel, kind),
        out_shape=(out,) * (NX - 1),
        in_specs=[spec(pltpu.SMEM)] * 2 + [spec(pl.ANY)] * NZ,
        out_specs=(spec(pltpu.VMEM),) * (NX - 1),
        scratch_shapes=[
            pltpu.VMEM((NZ * CODES, HD), jnp.bfloat16),
            pltpu.VMEM((NZ * 16, HD), jnp.bfloat16),
            pltpu.VMEM((SFAR, HD), jnp.float32),
            pltpu.VMEM((SFAR, HD), jnp.float32),
            pltpu.VMEM((TAKE, HD), jnp.float32),
            pltpu.VMEM((TAKE, HD), jnp.float32),
            pltpu.SemaphoreType.DMA((2 * NZ,)),
        ],
        name="pack",
    )(rows, marks, *parts)


def project_kernel(place, *refs):
    parts = refs[:8]
    gain, w_query, w_keyval, cosine, sine, q_out, k_out, v_out, qf = refs[8:]
    y, c = place[0], place[1]
    rows = parts[0].shape[0]
    width = parts[0].shape[1]
    power = jnp.zeros((rows, 1), jnp.float32)
    acc_q = jnp.zeros((rows, GROUP * HD), jnp.float32)
    acc_k = jnp.zeros((rows, HD), jnp.float32)
    acc_v = jnp.zeros((rows, HD), jnp.float32)
    for index, part in enumerate(parts):
        core = c if index < NY else 1 - c
        t = lax.rem(y + index % NY, NY) * 2 + core
        feats = part[...].astype(jnp.float32)
        power = power + jnp.sum(feats * feats, axis=1, keepdims=True)
        scaled = (feats * gain[pl.ds(t, 1), :]).astype(jnp.bfloat16)
        here = pl.ds(pl.multiple_of(t * width, width), width)
        acc_q = acc_q + jnp.dot(scaled, w_query[here, :], preferred_element_type=jnp.float32)
        acc_k = acc_k + jnp.dot(scaled, w_keyval[0, here, :], preferred_element_type=jnp.float32)
        acc_v = acc_v + jnp.dot(scaled, w_keyval[1, here, :], preferred_element_type=jnp.float32)
    norm = lax.rsqrt(power / (width * 8) + 1e-05)
    cos, sin = cosine[...], sine[...]

    def rope(v):
        return v * cos + pltpu.roll(v, HD // 2, 1) * sin

    for g in range(GROUP):
        head = rope(acc_q[:, g * HD : (g + 1) * HD] * norm) * HD ** (-0.5)
        qf[pl.ds(g, rows, stride=GROUP), :] = head
    q_out[...] = qf[...].astype(jnp.bfloat16)
    k_out[...] = rope(acc_k * norm).astype(jnp.bfloat16)
    v_out[...] = (acc_v * norm).astype(jnp.bfloat16)


def project(place, parts, gain, w_query, w_keyval, cosine, sine):
    rows = parts[0].shape[0]
    return pl.pallas_call(
        project_kernel,
        out_shape=(
            jax.ShapeDtypeStruct((rows * GROUP, HD), jnp.bfloat16),
            jax.ShapeDtypeStruct((rows, HD), jnp.bfloat16),
            jax.ShapeDtypeStruct((rows, HD), jnp.bfloat16),
        ),
        in_specs=[spec(pltpu.SMEM)] + [spec(pltpu.VMEM)] * 13,
        out_specs=(spec(pltpu.VMEM),) * 3,
        scratch_shapes=[pltpu.VMEM((rows * GROUP, HD), jnp.float32)],
        compiler_params=pltpu.CompilerParams(vmem_limit_bytes=LIMIT),
        name="project",
    )(place, *parts, gain, w_query, w_keyval, cosine, sine)


def load(parts, pool, sems):
    copies, at = [], 0
    for i, part in enumerate(parts):
        n = part.shape[0]
        copies.append(pltpu.make_async_copy(part, pool.at[pl.ds(at, n), :], sems.at[i]))
        copies[-1].start()
        at += n
    return copies


def pages(pool, where, slots):
    return jnp.concatenate(
        [pool[pl.ds(pl.multiple_of(where[s], 16), PAGE), :] for s in slots], axis=0
    )


def score_kernel(count, n, table, krow, mark, lens, q, k_new, v_new, own_scales, *refs):
    keys, refs = refs[:n], refs[n:]
    weights, fresh_out, pool, ksc, vsc, score, sems = refs
    copies = load(keys, pool, sems)
    for copy in copies:
        copy.wait()
    for part in range(NZ):
        both = pool[pl.ds(part * PART + 2 * CODES, 16), :].astype(jnp.float32)
        ksc[pl.ds(part * EXPORT, EXPORT), :] = both[:EXPORT]
        vsc[pl.ds(part * EXPORT, EXPORT), :] = both[EXPORT:]
    for part in range(NX - 1):
        at = FAR + part * KPACK + TAKE * PAGE
        ksc[pl.ds(SFAR + part * TAKE, TAKE), :] = pool[pl.ds(at, TAKE), :].astype(jnp.float32)
        vsc[pl.ds(SFAR + part * TAKE, TAKE), :] = pool[pl.ds(at + TAKE, TAKE), :].astype(
            jnp.float32
        )
    mine = own_scales[...].astype(jnp.float32)
    ksc[pl.ds(SOWN, OWN), :] = mine[:OWN]
    vsc[pl.ds(SOWN, OWN), :] = mine[OWN:]

    rows = BLOCK * ROWS
    span = 4 * PAGE
    lane = lax.broadcasted_iota(jnp.int32, (1, HD), 1)
    token = lax.broadcasted_iota(jnp.int32, (ROWS, span), 1)

    def scale_row(ref, slots):
        pieces = []
        for m in range(0, len(slots), 2):
            left = ref[pl.ds(mark[slots[m]], 1), :]
            right = ref[pl.ds(mark[slots[m + 1]], 1), :]
            pieces.append(jnp.where(lane < PAGE, left, right))
        return jnp.concatenate(pieces, axis=1)

    def one_block(block, carry):
        base = block * BLOCK
        here = pl.ds(pl.multiple_of(block * rows, rows), rows)
        queries = q[here, :]
        for i in range(BLOCK):
            branch = base + i
            length = lens[branch]
            for half in range(2):
                slots = [table[branch * MAXP + half * 4 + m] for m in range(4)]
                s = lax.dot_general(
                    queries[i * ROWS : (i + 1) * ROWS],
                    pages(pool, krow, slots),
                    (((1,), (1,)), ((), ())),
                    preferred_element_type=jnp.float32,
                )
                live = token < length - half * span
                score[pl.ds(i * ROWS, ROWS), pl.ds(half * span, span)] = jnp.where(
                    live, s * scale_row(ksc, slots), NEG
                )
        new = pl.ds(pl.multiple_of(base * STEPS, BLOCK * STEPS), BLOCK * STEPS)
        fresh = lax.dot_general(
            queries, k_new[new, :], (((1,), (1,)), ((), ())), preferred_element_type=jnp.float32
        )
        row = lax.broadcasted_iota(jnp.int32, fresh.shape, 0)
        col = lax.broadcasted_iota(jnp.int32, fresh.shape, 1)
        step = lax.shift_right_logical(row, 2)
        same = lax.shift_right_logical(step, 2) == lax.shift_right_logical(col, 2)
        fresh = jnp.where(same & ((step & 3) >= (col & 3)), fresh, NEG)
        context = score[...]
        top = jnp.maximum(
            jnp.max(context, axis=1, keepdims=True), jnp.max(fresh, axis=1, keepdims=True)
        )
        context = jnp.exp(context - top)
        fresh = jnp.exp(fresh - top)
        total = jnp.sum(context, axis=1, keepdims=True) + jnp.sum(fresh, axis=1, keepdims=True)
        inverse = 1.0 / total
        score[...] = context * inverse
        fresh_out[here, :] = jnp.dot(
            (fresh * inverse).astype(jnp.bfloat16),
            v_new[new, :],
            preferred_element_type=jnp.float32,
        )
        for i in range(BLOCK):
            branch = base + i
            slots = [table[branch * MAXP + m] for m in range(MAXP)]
            there = pl.ds(pl.multiple_of(block * rows + i * ROWS, ROWS), ROWS)
            weights[there, :] = (
                score[pl.ds(i * ROWS, ROWS), :] * scale_row(vsc, slots)
            ).astype(jnp.bfloat16)
        return carry

    lax.fori_loop(0, count // BLOCK, one_block, 0)


def score(table, krow, mark, lens, q, k_new, v_new, own_scales, keys):
    count = lens.shape[0]
    krows = sum(k.shape[0] for k in keys)
    return pl.pallas_call(
        functools.partial(score_kernel, count, len(keys)),
        out_shape=(
            jax.ShapeDtypeStruct((count * ROWS, MAXP * PAGE), jnp.bfloat16),
            jax.ShapeDtypeStruct((count * ROWS, HD), jnp.float32),
        ),
        in_specs=[spec(pltpu.SMEM)] * 4 + [spec(pltpu.VMEM)] * 4 + [spec(pl.ANY)] * len(keys),
        out_specs=(spec(pltpu.VMEM),) * 2,
        scratch_shapes=[
            pltpu.VMEM((krows, HD), jnp.bfloat16),
            pltpu.VMEM((SOWN + OWN, HD), jnp.float32),
            pltpu.VMEM((SOWN + OWN, HD), jnp.float32),
            pltpu.VMEM((BLOCK * ROWS, MAXP * PAGE), jnp.float32),
            pltpu.SemaphoreType.DMA((len(keys),)),
        ],
        compiler_params=pltpu.CompilerParams(vmem_limit_bytes=LIMIT),
        name="score",
    )(table, krow, mark, lens, q, k_new, v_new, own_scales, *keys)


def value_kernel(first, count, n, table, vrow, weights, fresh, *refs):
    values, (out, pool, result, sems) = refs[:n], refs[n:]
    copies = load(values, pool, sems)
    for copy in copies:
        copy.wait()

    def one_block(block, carry):
        for i in range(BLOCK):
            branch = first + block * BLOCK + i
            slots = [table[branch * MAXP + m] for m in range(MAXP)]
            here = pl.ds(pl.multiple_of((block * BLOCK + i) * ROWS, ROWS), ROWS)
            part = jnp.dot(
                weights[here, :], pages(pool, vrow, slots), preferred_element_type=jnp.float32
            )
            result[here, :] = part + fresh[here, :]
        return carry

    lax.fori_loop(0, count // BLOCK, one_block, 0)
    for g in range(GROUP):
        out[:, g * HD : (g + 1) * HD] = result[
            pl.ds(g, count * STEPS, stride=GROUP), :
        ].astype(jnp.bfloat16)


def value(first, count, table, vrow, weights, fresh, values):
    vrows = sum(v.shape[0] for v in values)
    chunk = first // count
    return pl.pallas_call(
        functools.partial(value_kernel, first, count, len(values)),
        grid=(1,),
        out_shape=jax.ShapeDtypeStruct((count * STEPS, GROUP * HD), jnp.bfloat16),
        in_specs=[spec(pltpu.SMEM)] * 2
        + [
            pl.BlockSpec((count * ROWS, MAXP * PAGE), lambda i: (chunk, 0)),
            pl.BlockSpec((count * ROWS, HD), lambda i: (chunk, 0)),
        ]
        + [spec(pl.ANY)] * len(values),
        out_specs=spec(pltpu.VMEM),
        scratch_shapes=[
            pltpu.VMEM((vrows, HD), jnp.bfloat16),
            pltpu.VMEM((count * ROWS, HD), jnp.float32),
            pltpu.SemaphoreType.DMA((len(values),)),
        ],
        compiler_params=pltpu.CompilerParams(vmem_limit_bytes=LIMIT),
        name="value",
    )(table, vrow, weights, fresh, *values)


def mix_kernel(place, near, far, w_near, w_far, *outs):
    y, c = place[0], place[1]
    half, width = outs[0].shape
    for j in (2, 1, 3, 0):
        at = pl.ds(pl.multiple_of((lax.rem(y + j, NY) * 2 + c) * width, width), width)
        total = jnp.dot(near[...], w_near[:, at], preferred_element_type=jnp.float32)
        total += jnp.dot(far[...], w_far[:, at], preferred_element_type=jnp.float32)
        outs[2 * j][...] = total[:half].astype(jnp.bfloat16)
        outs[2 * j + 1][...] = total[half:].astype(jnp.bfloat16)


def mix(place, near, far, w_near, w_far):
    width = w_near.shape[1] // (2 * NY)
    out = jax.ShapeDtypeStruct((near.shape[0] // 2, width), jnp.bfloat16)
    return pl.pallas_call(
        mix_kernel,
        out_shape=(out,) * (2 * NY),
        in_specs=[spec(pltpu.SMEM)] + [spec(pltpu.VMEM)] * 4,
        out_specs=(spec(pltpu.VMEM),) * (2 * NY),
        compiler_params=pltpu.CompilerParams(vmem_limit_bytes=LIMIT),
        name="mix",
    )(place, near, far, w_near, w_far)


def after(value, *others):
    return lax.optimization_barrier((value, *others))[0]


def plan_kernel(where, pull, rows, marks, krow, vrow, mark):
    z, x = where[0], where[1]

    def locate(j, side):
        name = pull[(z * NX + lax.rem(x + side, NX)) * FORK + j]
        source = lax.shift_right_logical(name, 3)
        dz = lax.shift_right_logical(source, 2) - z
        dx = (source & (NX - 1)) - x
        return name & (EXPORT - 1), dz & (NZ - 1), dx & (NX - 1)

    def clear(k, carry):
        rows[k] = 0
        marks[k] = 0
        return carry

    lax.fori_loop(0, (NX - 1) * TAKE, clear, 0, unroll=8)
    for side in range(1, NX):

        def send(j, count):
            entry, dz, dx = locate(j, side)
            match = dx == 0
            at = jnp.where(match, (side - 1) * TAKE + count, (NX - 1) * TAKE)
            rows[at] = dz * CODES + entry * PAGE
            marks[at] = dz * EXPORT + entry
            return count + match.astype(jnp.int32)

        lax.fori_loop(0, FORK, send, 0, unroll=8)

    def take(j, counts):
        entry, dz, dx = locate(j, 0)
        rank = jnp.where(dx == 1, counts[0], jnp.where(dx == 2, counts[1], counts[2]))
        near = dx == 0
        krow[j] = jnp.where(
            near, dz * PART + entry * PAGE, FAR + (dx - 1) * KPACK + rank * PAGE
        )
        mark[j] = jnp.where(near, dz * EXPORT + entry, SFAR + (dx - 1) * TAKE + rank)
        vrow[j] = jnp.where(
            near, dz * PART + CODES + entry * PAGE, FAR + (dx - 1) * VPACK + rank * PAGE
        )
        return tuple(counts[k] + (dx == k + 1).astype(jnp.int32) for k in range(NX - 1))

    zero = jnp.int32(0)
    lax.fori_loop(0, FORK, take, (zero,) * (NX - 1), unroll=8)

    def own(i, carry):
        krow[FORK + i] = KOWN + i * PAGE
        vrow[FORK + i] = VOWN + i * PAGE
        mark[FORK + i] = SOWN + i
        return carry

    lax.fori_loop(0, OWN, own, 0, unroll=8)


def plan(where, fork_pull):
    sends = jax.ShapeDtypeStruct(((NX - 1) * TAKE + 1,), jnp.int32)
    slots = jax.ShapeDtypeStruct((FORK + OWN,), jnp.int32)
    return pl.pallas_call(
        plan_kernel,
        out_shape=(sends, sends, slots, slots, slots),
        in_specs=[spec(pltpu.SMEM)] * 2,
        out_specs=(spec(pltpu.SMEM),) * 5,
        name="plan",
    )(where, fork_pull.reshape(-1))


def per_device(
    hidden,
    gain,
    w_query,
    w_keyval,
    w_out,
    kv_codes,
    kv_scales,
    fork_export,
    fork_pull,
    page_table,
    lengths,
):
    branches, steps, width = hidden.shape
    rows = branches * steps
    tensor = lax.axis_index("tensor")
    myself = lax.axis_index("branch")
    place = jnp.stack([tensor // 2, tensor % 2]).astype(jnp.int32)

    where = jnp.stack([myself // NX, myself % NX]).astype(jnp.int32)
    part = export_pages(kv_codes, kv_scales.transpose(2, 1, 0).reshape(2, OWN), fork_export)
    own = after(hidden, part).reshape(rows, width)
    z = {0: part, 1: from_z(part, 1, "pages1"), -1: from_z(part, -1, "pages1")}
    aside = [from_y(own, d, "hidden") for d in (1, 2, 3)]
    w_far = from_core(w_out, "w_out")
    z[2] = from_z(after(z[1], w_far), 1, "pages2")
    z[-2] = from_z(after(z[-1], w_far), -1, "pages2")
    half = HD // 2
    freq = jnp.exp(-(2.0 * jnp.arange(half).astype(jnp.float32) / HD) * math.log(500000.0))
    positions = (after(lengths, z[1], z[-1])[:, None] + jnp.arange(steps, dtype=jnp.int32)[None, :]).reshape(-1)
    angle = positions.astype(jnp.float32)[:, None] * freq[None, :]
    cos, sin = jnp.cos(angle), jnp.sin(angle)
    cosine = jnp.concatenate([cos, cos], axis=1)
    sine = jnp.concatenate([-sin, sin], axis=1)
    z[2], z[-2] = after(z[2], cosine, sine), after(z[-2], cosine, sine)
    z[3], z[-3] = from_z(z[2], 1, "pages3"), from_z(z[-2], -1, "pages3")
    z[4] = from_z(after(z[3], z[-3]), 1, "pages4")
    where = after(where, z[3], z[-3])
    send_rows, send_marks, krow, vrow, mark = plan(where, fork_pull)
    plus_far, across_far = [
        from_core(after(aside[i], z[2], z[-2]), "hidden_core") for i in (0, 1)
    ]
    column = [z[d] for d in (0, 1, 2, 3, 4, -3, -2, -1)]
    column[0] = after(column[0], plus_far, across_far)

    def sides(plus, across, minus, name):
        return [from_x(minus, 1, name), from_x(across, 2, name), from_x(plus, -1, name)]

    packed = pack(0, send_rows, send_marks, column)
    keys = column + sides(*packed, "key_side")
    minus_far = from_core(after(aside[2], *packed), "hidden_core")
    own_far = from_core(after(own, *packed), "hidden_core")
    column[0] = after(column[0], *packed, minus_far, own_far)
    plus, across, minus = pack(1, send_rows, send_marks, column)
    parts = [own, *aside, own_far, plus_far, across_far, minus_far]

    q, k_new, v_new = project(
        place, parts, gain.reshape(2 * NY, width), w_query, w_keyval, cosine, sine
    )

    keys = keys + [kv_codes[:, 0].reshape(OWN * PAGE, HD)]
    own_scales = jnp.broadcast_to(
        jnp.transpose(kv_scales, (1, 0, 2)).reshape(2 * OWN, 1), (2 * OWN, HD)
    )
    table = page_table.reshape(-1)

    across = after(across, q)
    values = column + sides(plus, across, minus, "value_side")
    values = values + [kv_codes[:, 1].reshape(OWN * PAGE, HD)]
    weights, fresh = score(table, krow, mark, lengths, q, k_new, v_new, own_scales, keys)
    attended = value(0, branches, table, vrow, weights, fresh, values)
    other = from_core(attended, "attended_core")
    own_up, own_low, plus_up, plus_low, across_up, across_low, minus_up, minus_low = mix(
        place, attended, other, w_out, w_far
    )

    def add(*terms):
        total = terms[0].astype(jnp.float32)
        for term in terms[1:]:
            total = total + term.astype(jnp.float32)
        return total.astype(jnp.bfloat16)

    passed_up = from_y(across_up, -1, "output_relay")
    passed_low = from_y(across_low, 1, "output_relay")
    got_low = from_y(plus_low, -1, "output_near")
    got_up = from_y(minus_up, 1, "output_near")
    relayed_up = from_y(add(plus_up, passed_up), -1, "output_far")
    relayed_low = from_y(add(minus_low, passed_low), 1, "output_far")
    up = add(own_up, got_up, relayed_up).reshape(branches // 2, steps, width)
    low = add(own_low, got_low, relayed_low).reshape(branches // 2, steps, width)
    return jnp.concatenate([up, low], axis=0)


def solution(mesh):
    return jax.shard_map(
        per_device,
        mesh=mesh,
        in_specs=(
            P("branch", None, "tensor"),
            P(),
            P(None, "tensor"),
            P(None, None, "tensor"),
            P("tensor", None),
            P("branch", None, None, "tensor"),
            P("branch", None, "tensor"),
            P("branch"),
            P(),
            P("branch", None),
            P("branch"),
        ),
        out_specs=P("branch", None, "tensor"),
        check_vma=False,
    )
```

```python
import functools
import math

import jax
import jax.numpy as jnp
from jax import lax
from jax.experimental import pallas as pl
from jax.experimental.pallas import tpu as pltpu
from jax.sharding import PartitionSpec as P

HEADS = 32
KVH = 8
HD = 128
PAGE = 64
MAXP = 8
STEPS = 4
GROUP = HEADS // KVH
OWN = 32
FORK = 64
EXPORT = 8
NZ, NX, NY = 8, 4, 4
ROWS = GROUP * STEPS
CODES = EXPORT * PAGE
PART = 2 * CODES + 16
TAKE = NZ * 4
FAR = NZ * PART
KPACK = TAKE * PAGE + 2 * TAKE
VPACK = TAKE * PAGE
KOWN = FAR + (NX - 1) * KPACK
VOWN = FAR + (NX - 1) * VPACK
SFAR = NZ * EXPORT
SOWN = SFAR + (NX - 1) * TAKE
BLOCK = 16
NEG = -1e30
LIMIT = 30 * 1024 * 1024


def from_z(value, d, name="z"):
    perm = [(z * NX + x, ((z - d) % NZ) * NX + x) for z in range(NZ) for x in range(NX)]
    with jax.named_scope(name):
        return lax.ppermute(value, "branch", perm)


def from_x(value, d, name="x"):
    perm = [(z * NX + x, z * NX + (x - d) % NX) for z in range(NZ) for x in range(NX)]
    with jax.named_scope(name):
        return lax.ppermute(value, "branch", perm)


def from_y(value, d, name="y"):
    perm = [(y * 2 + c, ((y - d) % NY) * 2 + c) for y in range(NY) for c in range(2)]
    with jax.named_scope(name):
        return lax.ppermute(value, "tensor", perm)


def from_core(value, name="core"):
    with jax.named_scope(name):
        return lax.ppermute(value, "tensor", [(t, t ^ 1) for t in range(2 * NY)])


def spec(space):
    return pl.BlockSpec(memory_space=space)


def export_kernel(picks, scales, codes, out, sems):
    copies = []
    for e in range(EXPORT):
        page = picks[e]
        for kind in range(2):
            rows = pl.ds(kind * CODES + e * PAGE, PAGE)
            copies.append(
                pltpu.make_async_copy(codes.at[page, kind], out.at[rows, :], sems.at[2 * e + kind])
            )
            copies[-1].start()
    place = lax.broadcasted_iota(jnp.int32, (16, HD), 0)
    rows = jnp.zeros((16, HD), jnp.float32)
    table = scales[...].astype(jnp.float32)
    lane = lax.broadcasted_iota(jnp.int32, table.shape, 1)
    for e in range(EXPORT):
        pair = jnp.sum(jnp.where(lane == picks[e], table, 0.0), axis=1, keepdims=True)
        for kind in range(2):
            rows = jnp.where(place == kind * EXPORT + e, pair[kind : kind + 1, :], rows)
    out[pl.ds(2 * CODES, 16), :] = rows.astype(jnp.bfloat16)
    for copy in copies:
        copy.wait()


def export_pages(codes, scales, picks):
    return pl.pallas_call(
        export_kernel,
        out_shape=jax.ShapeDtypeStruct((PART, HD), jnp.bfloat16),
        in_specs=[spec(pltpu.SMEM), spec(pltpu.VMEM), spec(pl.ANY)],
        out_specs=spec(pltpu.VMEM),
        scratch_shapes=[pltpu.SemaphoreType.DMA((2 * EXPORT,))],
        name="export_pages",
    )(picks, scales, codes)


def pack_kernel(kind, rows, marks, *refs):
    parts, outs = refs[:NZ], refs[NZ : NZ + NX - 1]
    pool, both, ksc, vsc, kout, vout, sems = refs[NZ + NX - 1 :]
    copies = []
    for i, part in enumerate(parts):
        ends = ((part, kind * CODES, pool, CODES), (part, 2 * CODES, both, 16))
        for source, at, target, n in ends[: 2 - kind]:
            to = target.at[pl.ds(i * n, n), :]
            sem = sems.at[2 * i + (target is both)]
            copies.append(pltpu.make_async_copy(source.at[pl.ds(at, n), :], to, sem))
            copies[-1].start()
    for copy in copies:
        copy.wait()
    if kind == 0:
        for i in range(NZ):
            pair = both[pl.ds(i * 16, 16), :].astype(jnp.float32)
            ksc[pl.ds(i * EXPORT, EXPORT), :] = pair[:EXPORT]
            vsc[pl.ds(i * EXPORT, EXPORT), :] = pair[EXPORT:]
    for d, out in enumerate(outs):
        for k in range(TAKE):
            row = pl.multiple_of(rows[d * TAKE + k], 16)
            out[pl.ds(k * PAGE, PAGE), :] = pool[pl.ds(row, PAGE), :]
        if kind == 0:
            for k in range(TAKE):
                mark = marks[d * TAKE + k]
                kout[pl.ds(k, 1), :] = ksc[pl.ds(mark, 1), :]
                vout[pl.ds(k, 1), :] = vsc[pl.ds(mark, 1), :]
            out[pl.ds(TAKE * PAGE, TAKE), :] = kout[...].astype(jnp.bfloat16)
            out[pl.ds(TAKE * PAGE + TAKE, TAKE), :] = vout[...].astype(jnp.bfloat16)


def pack(kind, rows, marks, parts):
    out = jax.ShapeDtypeStruct((VPACK if kind else KPACK, HD), jnp.bfloat16)
    return pl.pallas_call(
        functools.partial(pack_kernel, kind),
        out_shape=(out,) * (NX - 1),
        in_specs=[spec(pltpu.SMEM)] * 2 + [spec(pl.ANY)] * NZ,
        out_specs=(spec(pltpu.VMEM),) * (NX - 1),
        scratch_shapes=[
            pltpu.VMEM((NZ * CODES, HD), jnp.bfloat16),
            pltpu.VMEM((NZ * 16, HD), jnp.bfloat16),
            pltpu.VMEM((SFAR, HD), jnp.float32),
            pltpu.VMEM((SFAR, HD), jnp.float32),
            pltpu.VMEM((TAKE, HD), jnp.float32),
            pltpu.VMEM((TAKE, HD), jnp.float32),
            pltpu.SemaphoreType.DMA((2 * NZ,)),
        ],
        name="pack",
    )(rows, marks, *parts)


def project_kernel(place, *refs):
    parts = refs[:8]
    gain, w_query, w_keyval, cosine, sine, q_out, k_out, v_out, qf = refs[8:]
    y, c = place[0], place[1]
    rows = parts[0].shape[0]
    width = parts[0].shape[1]
    power = jnp.zeros((rows, 1), jnp.float32)
    acc_q = jnp.zeros((rows, GROUP * HD), jnp.float32)
    acc_k = jnp.zeros((rows, HD), jnp.float32)
    acc_v = jnp.zeros((rows, HD), jnp.float32)
    for index, part in enumerate(parts):
        core = c if index < NY else 1 - c
        t = lax.rem(y + index % NY, NY) * 2 + core
        feats = part[...].astype(jnp.float32)
        power = power + jnp.sum(feats * feats, axis=1, keepdims=True)
        scaled = (feats * gain[pl.ds(t, 1), :]).astype(jnp.bfloat16)
        here = pl.ds(pl.multiple_of(t * width, width), width)
        acc_q = acc_q + jnp.dot(scaled, w_query[here, :], preferred_element_type=jnp.float32)
        acc_k = acc_k + jnp.dot(scaled, w_keyval[0, here, :], preferred_element_type=jnp.float32)
        acc_v = acc_v + jnp.dot(scaled, w_keyval[1, here, :], preferred_element_type=jnp.float32)
    norm = lax.rsqrt(power / (width * 8) + 1e-05)
    cos, sin = cosine[...], sine[...]

    def rope(v):
        return v * cos + pltpu.roll(v, HD // 2, 1) * sin

    for g in range(GROUP):
        head = rope(acc_q[:, g * HD : (g + 1) * HD] * norm) * HD ** (-0.5)
        qf[pl.ds(g, rows, stride=GROUP), :] = head
    q_out[...] = qf[...].astype(jnp.bfloat16)
    k_out[...] = rope(acc_k * norm).astype(jnp.bfloat16)
    v_out[...] = (acc_v * norm).astype(jnp.bfloat16)


def project(place, parts, gain, w_query, w_keyval, cosine, sine):
    rows = parts[0].shape[0]
    return pl.pallas_call(
        project_kernel,
        out_shape=(
            jax.ShapeDtypeStruct((rows * GROUP, HD), jnp.bfloat16),
            jax.ShapeDtypeStruct((rows, HD), jnp.bfloat16),
            jax.ShapeDtypeStruct((rows, HD), jnp.bfloat16),
        ),
        in_specs=[spec(pltpu.SMEM)] + [spec(pltpu.VMEM)] * 13,
        out_specs=(spec(pltpu.VMEM),) * 3,
        scratch_shapes=[pltpu.VMEM((rows * GROUP, HD), jnp.float32)],
        compiler_params=pltpu.CompilerParams(vmem_limit_bytes=LIMIT),
        name="project",
    )(place, *parts, gain, w_query, w_keyval, cosine, sine)


def load(parts, pool, sems):
    copies, at = [], 0
    for i, part in enumerate(parts):
        n = part.shape[0]
        copies.append(pltpu.make_async_copy(part, pool.at[pl.ds(at, n), :], sems.at[i]))
        copies[-1].start()
        at += n
    return copies


def pages(pool, where, slots):
    return jnp.concatenate(
        [pool[pl.ds(pl.multiple_of(where[s], 16), PAGE), :] for s in slots], axis=0
    )


def score_kernel(count, n, table, krow, mark, lens, q, k_new, v_new, own_scales, *refs):
    keys, refs = refs[:n], refs[n:]
    weights, fresh_out, pool, ksc, vsc, score, sems = refs
    copies = load(keys, pool, sems)
    for copy in copies:
        copy.wait()
    for part in range(NZ):
        both = pool[pl.ds(part * PART + 2 * CODES, 16), :].astype(jnp.float32)
        ksc[pl.ds(part * EXPORT, EXPORT), :] = both[:EXPORT]
        vsc[pl.ds(part * EXPORT, EXPORT), :] = both[EXPORT:]
    for part in range(NX - 1):
        at = FAR + part * KPACK + TAKE * PAGE
        ksc[pl.ds(SFAR + part * TAKE, TAKE), :] = pool[pl.ds(at, TAKE), :].astype(jnp.float32)
        vsc[pl.ds(SFAR + part * TAKE, TAKE), :] = pool[pl.ds(at + TAKE, TAKE), :].astype(
            jnp.float32
        )
    mine = own_scales[...].astype(jnp.float32)
    ksc[pl.ds(SOWN, OWN), :] = mine[:OWN]
    vsc[pl.ds(SOWN, OWN), :] = mine[OWN:]

    rows = BLOCK * ROWS
    span = 4 * PAGE
    lane = lax.broadcasted_iota(jnp.int32, (1, HD), 1)
    token = lax.broadcasted_iota(jnp.int32, (ROWS, span), 1)

    def scale_row(ref, slots):
        pieces = []
        for m in range(0, len(slots), 2):
            left = ref[pl.ds(mark[slots[m]], 1), :]
            right = ref[pl.ds(mark[slots[m + 1]], 1), :]
            pieces.append(jnp.where(lane < PAGE, left, right))
        return jnp.concatenate(pieces, axis=1)

    def one_block(block, carry):
        base = block * BLOCK
        here = pl.ds(pl.multiple_of(block * rows, rows), rows)
        queries = q[here, :]
        for i in range(BLOCK):
            branch = base + i
            length = lens[branch]
            for half in range(2):
                slots = [table[branch * MAXP + half * 4 + m] for m in range(4)]
                s = lax.dot_general(
                    queries[i * ROWS : (i + 1) * ROWS],
                    pages(pool, krow, slots),
                    (((1,), (1,)), ((), ())),
                    preferred_element_type=jnp.float32,
                )
                live = token < length - half * span
                score[pl.ds(i * ROWS, ROWS), pl.ds(half * span, span)] = jnp.where(
                    live, s * scale_row(ksc, slots), NEG
                )
        new = pl.ds(pl.multiple_of(base * STEPS, BLOCK * STEPS), BLOCK * STEPS)
        fresh = lax.dot_general(
            queries, k_new[new, :], (((1,), (1,)), ((), ())), preferred_element_type=jnp.float32
        )
        row = lax.broadcasted_iota(jnp.int32, fresh.shape, 0)
        col = lax.broadcasted_iota(jnp.int32, fresh.shape, 1)
        step = lax.shift_right_logical(row, 2)
        same = lax.shift_right_logical(step, 2) == lax.shift_right_logical(col, 2)
        fresh = jnp.where(same & ((step & 3) >= (col & 3)), fresh, NEG)
        context = score[...]
        top = jnp.maximum(
            jnp.max(context, axis=1, keepdims=True), jnp.max(fresh, axis=1, keepdims=True)
        )
        context = jnp.exp(context - top)
        fresh = jnp.exp(fresh - top)
        total = jnp.sum(context, axis=1, keepdims=True) + jnp.sum(fresh, axis=1, keepdims=True)
        inverse = 1.0 / total
        score[...] = context * inverse
        fresh_out[here, :] = jnp.dot(
            (fresh * inverse).astype(jnp.bfloat16),
            v_new[new, :],
            preferred_element_type=jnp.float32,
        )
        for i in range(BLOCK):
            branch = base + i
            slots = [table[branch * MAXP + m] for m in range(MAXP)]
            there = pl.ds(pl.multiple_of(block * rows + i * ROWS, ROWS), ROWS)
            weights[there, :] = (
                score[pl.ds(i * ROWS, ROWS), :] * scale_row(vsc, slots)
            ).astype(jnp.bfloat16)
        return carry

    lax.fori_loop(0, count // BLOCK, one_block, 0)


def score(table, krow, mark, lens, q, k_new, v_new, own_scales, keys):
    count = lens.shape[0]
    krows = sum(k.shape[0] for k in keys)
    return pl.pallas_call(
        functools.partial(score_kernel, count, len(keys)),
        out_shape=(
            jax.ShapeDtypeStruct((count * ROWS, MAXP * PAGE), jnp.bfloat16),
            jax.ShapeDtypeStruct((count * ROWS, HD), jnp.float32),
        ),
        in_specs=[spec(pltpu.SMEM)] * 4 + [spec(pltpu.VMEM)] * 4 + [spec(pl.ANY)] * len(keys),
        out_specs=(spec(pltpu.VMEM),) * 2,
        scratch_shapes=[
            pltpu.VMEM((krows, HD), jnp.bfloat16),
            pltpu.VMEM((SOWN + OWN, HD), jnp.float32),
            pltpu.VMEM((SOWN + OWN, HD), jnp.float32),
            pltpu.VMEM((BLOCK * ROWS, MAXP * PAGE), jnp.float32),
            pltpu.SemaphoreType.DMA((len(keys),)),
        ],
        compiler_params=pltpu.CompilerParams(vmem_limit_bytes=LIMIT),
        name="score",
    )(table, krow, mark, lens, q, k_new, v_new, own_scales, *keys)


def value_kernel(first, count, n, table, vrow, weights, fresh, *refs):
    values, (out, pool, result, sems) = refs[:n], refs[n:]
    copies = load(values, pool, sems)
    for copy in copies:
        copy.wait()

    def one_block(block, carry):
        for i in range(BLOCK):
            branch = first + block * BLOCK + i
            slots = [table[branch * MAXP + m] for m in range(MAXP)]
            here = pl.ds(pl.multiple_of((block * BLOCK + i) * ROWS, ROWS), ROWS)
            part = jnp.dot(
                weights[here, :], pages(pool, vrow, slots), preferred_element_type=jnp.float32
            )
            result[here, :] = part + fresh[here, :]
        return carry

    lax.fori_loop(0, count // BLOCK, one_block, 0)
    for g in range(GROUP):
        out[:, g * HD : (g + 1) * HD] = result[
            pl.ds(g, count * STEPS, stride=GROUP), :
        ].astype(jnp.bfloat16)


def value(first, count, table, vrow, weights, fresh, values):
    vrows = sum(v.shape[0] for v in values)
    chunk = first // count
    return pl.pallas_call(
        functools.partial(value_kernel, first, count, len(values)),
        grid=(1,),
        out_shape=jax.ShapeDtypeStruct((count * STEPS, GROUP * HD), jnp.bfloat16),
        in_specs=[spec(pltpu.SMEM)] * 2
        + [
            pl.BlockSpec((count * ROWS, MAXP * PAGE), lambda i: (chunk, 0)),
            pl.BlockSpec((count * ROWS, HD), lambda i: (chunk, 0)),
        ]
        + [spec(pl.ANY)] * len(values),
        out_specs=spec(pltpu.VMEM),
        scratch_shapes=[
            pltpu.VMEM((vrows, HD), jnp.bfloat16),
            pltpu.VMEM((count * ROWS, HD), jnp.float32),
            pltpu.SemaphoreType.DMA((len(values),)),
        ],
        compiler_params=pltpu.CompilerParams(vmem_limit_bytes=LIMIT),
        name="value",
    )(table, vrow, weights, fresh, *values)


def mix_kernel(blocks, place, near, far, w_near, w_far, *outs):
    y, c = place[0], place[1]
    half, width = outs[0].shape
    for i, j in enumerate(blocks):
        at = pl.ds(pl.multiple_of((lax.rem(y + j, NY) * 2 + c) * width, width), width)
        total = jnp.dot(near[...], w_near[:, at], preferred_element_type=jnp.float32)
        total += jnp.dot(far[...], w_far[:, at], preferred_element_type=jnp.float32)
        outs[2 * i][...] = total[:half].astype(jnp.bfloat16)
        outs[2 * i + 1][...] = total[half:].astype(jnp.bfloat16)


def mix(blocks, place, near, far, w_near, w_far):
    width = w_near.shape[1] // (2 * NY)
    out = jax.ShapeDtypeStruct((near.shape[0] // 2, width), jnp.bfloat16)
    return pl.pallas_call(
        functools.partial(mix_kernel, blocks),
        out_shape=(out,) * (2 * len(blocks)),
        in_specs=[spec(pltpu.SMEM)] + [spec(pltpu.VMEM)] * 4,
        out_specs=(spec(pltpu.VMEM),) * (2 * len(blocks)),
        compiler_params=pltpu.CompilerParams(vmem_limit_bytes=LIMIT),
        name="mix",
    )(place, near, far, w_near, w_far)


def after(value, *others):
    return lax.optimization_barrier((value, *others))[0]


def plan_kernel(where, pull, rows, marks, krow, vrow, mark):
    z, x = where[0], where[1]

    def locate(j, side):
        name = pull[(z * NX + lax.rem(x + side, NX)) * FORK + j]
        source = lax.shift_right_logical(name, 3)
        dz = lax.shift_right_logical(source, 2) - z
        dx = (source & (NX - 1)) - x
        return name & (EXPORT - 1), dz & (NZ - 1), dx & (NX - 1)

    def clear(k, carry):
        rows[k] = 0
        marks[k] = 0
        return carry

    lax.fori_loop(0, (NX - 1) * TAKE, clear, 0, unroll=8)
    for side in range(1, NX):

        def send(j, count):
            entry, dz, dx = locate(j, side)
            match = dx == 0
            at = jnp.where(match, (side - 1) * TAKE + count, (NX - 1) * TAKE)
            rows[at] = dz * CODES + entry * PAGE
            marks[at] = dz * EXPORT + entry
            return count + match.astype(jnp.int32)

        lax.fori_loop(0, FORK, send, 0, unroll=8)

    def take(j, counts):
        entry, dz, dx = locate(j, 0)
        rank = jnp.where(dx == 1, counts[0], jnp.where(dx == 2, counts[1], counts[2]))
        near = dx == 0
        krow[j] = jnp.where(
            near, dz * PART + entry * PAGE, FAR + (dx - 1) * KPACK + rank * PAGE
        )
        mark[j] = jnp.where(near, dz * EXPORT + entry, SFAR + (dx - 1) * TAKE + rank)
        vrow[j] = jnp.where(
            near, dz * PART + CODES + entry * PAGE, FAR + (dx - 1) * VPACK + rank * PAGE
        )
        return tuple(counts[k] + (dx == k + 1).astype(jnp.int32) for k in range(NX - 1))

    zero = jnp.int32(0)
    lax.fori_loop(0, FORK, take, (zero,) * (NX - 1), unroll=8)

    def own(i, carry):
        krow[FORK + i] = KOWN + i * PAGE
        vrow[FORK + i] = VOWN + i * PAGE
        mark[FORK + i] = SOWN + i
        return carry

    lax.fori_loop(0, OWN, own, 0, unroll=8)


def plan(where, fork_pull):
    sends = jax.ShapeDtypeStruct(((NX - 1) * TAKE + 1,), jnp.int32)
    slots = jax.ShapeDtypeStruct((FORK + OWN,), jnp.int32)
    return pl.pallas_call(
        plan_kernel,
        out_shape=(sends, sends, slots, slots, slots),
        in_specs=[spec(pltpu.SMEM)] * 2,
        out_specs=(spec(pltpu.SMEM),) * 5,
        name="plan",
    )(where, fork_pull.reshape(-1))


def per_device(
    hidden,
    gain,
    w_query,
    w_keyval,
    w_out,
    kv_codes,
    kv_scales,
    fork_export,
    fork_pull,
    page_table,
    lengths,
):
    branches, steps, width = hidden.shape
    rows = branches * steps
    tensor = lax.axis_index("tensor")
    myself = lax.axis_index("branch")
    place = jnp.stack([tensor // 2, tensor % 2]).astype(jnp.int32)

    where = jnp.stack([myself // NX, myself % NX]).astype(jnp.int32)
    part = export_pages(kv_codes, kv_scales.transpose(2, 1, 0).reshape(2, OWN), fork_export)
    own = after(hidden, part).reshape(rows, width)
    z = {0: part, 1: from_z(part, 1, "pages1"), -1: from_z(part, -1, "pages1")}
    aside = [from_y(own, d, "hidden") for d in (1, 2, 3)]
    w_far = from_core(w_out, "w_out")
    z[2] = from_z(after(z[1], w_far), 1, "pages2")
    z[-2] = from_z(after(z[-1], w_far), -1, "pages2")
    half = HD // 2
    freq = jnp.exp(-(2.0 * jnp.arange(half).astype(jnp.float32) / HD) * math.log(500000.0))
    positions = (after(lengths, z[1], z[-1])[:, None] + jnp.arange(steps, dtype=jnp.int32)[None, :]).reshape(-1)
    angle = positions.astype(jnp.float32)[:, None] * freq[None, :]
    cos, sin = jnp.cos(angle), jnp.sin(angle)
    cosine = jnp.concatenate([cos, cos], axis=1)
    sine = jnp.concatenate([-sin, sin], axis=1)
    z[2], z[-2] = after(z[2], cosine, sine), after(z[-2], cosine, sine)
    z[3], z[-3] = from_z(z[2], 1, "pages3"), from_z(z[-2], -1, "pages3")
    z[4] = from_z(after(z[3], z[-3]), 1, "pages4")
    where = after(where, z[3], z[-3])
    send_rows, send_marks, krow, vrow, mark = plan(where, fork_pull)
    plus_far, across_far = [
        from_core(after(aside[i], z[2], z[-2]), "hidden_core") for i in (0, 1)
    ]
    column = [z[d] for d in (0, 1, 2, 3, 4, -3, -2, -1)]
    column[0] = after(column[0], plus_far, across_far)

    def sides(plus, across, minus, name):
        return [from_x(minus, 1, name), from_x(across, 2, name), from_x(plus, -1, name)]

    packed = pack(0, send_rows, send_marks, column)
    keys = column + sides(*packed, "key_side")
    minus_far = from_core(after(aside[2], *packed), "hidden_core")
    own_far = from_core(after(own, *packed), "hidden_core")
    column[0] = after(column[0], *packed, minus_far, own_far)
    plus, across, minus = pack(1, send_rows, send_marks, column)
    parts = [own, *aside, own_far, plus_far, across_far, minus_far]

    q, k_new, v_new = project(
        place, parts, gain.reshape(2 * NY, width), w_query, w_keyval, cosine, sine
    )

    keys = keys + [kv_codes[:, 0].reshape(OWN * PAGE, HD)]
    own_scales = jnp.broadcast_to(
        jnp.transpose(kv_scales, (1, 0, 2)).reshape(2 * OWN, 1), (2 * OWN, HD)
    )
    table = page_table.reshape(-1)

    across = after(across, q)
    values = column + sides(plus, across, minus, "value_side")
    values = values + [kv_codes[:, 1].reshape(OWN * PAGE, HD)]
    weights, fresh = score(table, krow, mark, lengths, q, k_new, v_new, own_scales, keys)
    attended = value(0, branches, table, vrow, weights, fresh, values)
    other = from_core(attended, "attended_core")
    across_up, across_low = mix((2,), place, attended, other, w_out, w_far)
    passed_up = from_y(across_up, -1, "output_relay")
    passed_low = from_y(across_low, 1, "output_relay")
    attended = after(attended, across_up)
    plus_up, plus_low, minus_up, minus_low, own_up, own_low = mix(
        (1, 3, 0), place, attended, other, w_out, w_far
    )

    def add(*terms):
        total = terms[0].astype(jnp.float32)
        for term in terms[1:]:
            total = total + term.astype(jnp.float32)
        return total.astype(jnp.bfloat16)

    got_low = from_y(plus_low, -1, "output_near")
    got_up = from_y(minus_up, 1, "output_near")
    relayed_up = from_y(add(plus_up, passed_up), -1, "output_far")
    relayed_low = from_y(add(minus_low, passed_low), 1, "output_far")
    up = add(own_up, got_up, relayed_up).reshape(branches // 2, steps, width)
    low = add(own_low, got_low, relayed_low).reshape(branches // 2, steps, width)
    return jnp.concatenate([up, low], axis=0)


def solution(mesh):
    return jax.shard_map(
        per_device,
        mesh=mesh,
        in_specs=(
            P("branch", None, "tensor"),
            P(),
            P(None, "tensor"),
            P(None, None, "tensor"),
            P("tensor", None),
            P("branch", None, None, "tensor"),
            P("branch", None, "tensor"),
            P("branch"),
            P(),
            P("branch", None),
            P("branch"),
        ),
        out_specs=P("branch", None, "tensor"),
        check_vma=False,
    )
```
